128 devices in a mesh: gx: 8 (over x, core), gy: 16 (over y, z).
Axes of the slice: x: 4, y: 4, z: 4, core: 2. Of those that a mesh axis runs over, the one named last changes fastest.
Arguments:
- pressure_source: float32 [192, 384, 384], P('gx', 'gy'), may hold values from -6 to 6
- building_heights: int32 [32, 64], replicated, may hold values from 0 to 63
Outputs:
- correction: float32 [192, 384, 384], P('gx', 'gy')
- coarse_solution: float32 [64, 128, 128], P('gx', 'gy')
The draws below stay inside these ranges and needn't reach their ends.
Inputs may be any that keep to these rules, and one draw needn't show every extreme that they name: `building_heights`: the height of the building in each element column, in elements, so that the top layer of every column is fluid.
All inputs are finite; a program needn't handle non-finite values.
Results may differ from the reference program's by a relative error of at most 0.0003.
Values sent between devices are 32-bit elements; how exact they have to be, the bound alone decides.
No kernel may reach another device: no remote copies, remote signals or barrier semaphores. Data moves between devices by JAX's collectives and lax.ppermute only.
A program may use at most 128 MiB of HBM per device.

```python
import jax
import jax.numpy as jnp
import numpy as np
from jax import lax

EC = 64
CG_ITERS = 10
NA = 32
NB = 64


def plant(drawn, own_key, low, largest):
    longest = drawn.shape.index(max(drawn.shape))
    spots = []
    for shift in (0, 1):
        where = [jax.random.randint(jax.random.fold_in(own_key, axis), (), 0, length) for axis, length in enumerate(drawn.shape)]
        where[longest] = (where[longest] + shift) % drawn.shape[longest]
        spots.append(tuple(where))
    return drawn.at[spots[0]].set(low).at[spots[1]].set(largest)


def block_levels(stream_key, extent, split, smallest, largest):
    def one(dim, parts):
        heights = jax.random.uniform(jax.random.fold_in(jax.random.fold_in(stream_key, 6), dim), (parts,), jnp.float32, smallest / len(split), largest / len(split))
        return jnp.repeat(jnp.exp(heights), extent[dim] // parts).reshape((-1,) + (1,) * (len(extent) - dim - 1))

    gain = one(*split[0])
    for cut in split[1:]:
        gain = gain * one(*cut)
    return gain


def gaussian(stream_key, shape, scale, reach, cuts=(), held_as=jnp.bfloat16):
    level = block_levels(stream_key, shape, cuts, -0.22, 0.18) if cuts else 1.0
    values = jax.random.normal(stream_key, shape, jnp.float32) * scale * level
    return jnp.minimum(jnp.maximum(values, -reach), reach).astype(held_as)


def setup_inputs(seed: int = 0) -> dict:
    splits = jax.random.split(jax.random.key(seed), 3)
    pressure_source = gaussian(splits[0], (6 * NA, 6 * NB, 6 * EC), 1.0, 6.0, ((0, 8), (1, 16)), jnp.float32)
    building_heights = plant(jax.random.randint(splits[1], (NA, NB), 0, EC), jax.random.fold_in(splits[1], 1), 0, EC - 1).astype(jnp.int32)
    return {"pressure_source": pressure_source, "building_heights": building_heights}


HIGHEST = lax.Precision.HIGHEST


def gll_nodes(node_count):
    if node_count == 6:
        outer_point = 0.7650553239294647
        inner_point = 0.2852315164806451
        points = [-1.0, -outer_point, -inner_point, inner_point, outer_point, 1.0]
        weights = [1.0 / 15.0, 0.3784749562978470, 0.5548583770354863, 0.5548583770354863, 0.3784749562978470, 1.0 / 15.0]
    elif node_count == 4:
        inner_point = 0.4472135954999579
        points = [-1.0, -inner_point, inner_point, 1.0]
        weights = [1.0 / 6.0, 5.0 / 6.0, 5.0 / 6.0, 1.0 / 6.0]
    else:
        points = [-1.0, 1.0]
        weights = [1.0, 1.0]
    return np.array(points), np.array(weights)


def diagonal_of(matrix):
    return np.array([matrix[index_id, index_id] for index_id in range(matrix.shape[0])])


def lagrange_tables(node_count):
    points, weights = gll_nodes(node_count)
    others = [[points[col_id] - points[other] for other in range(node_count) if other != col_id] for col_id in range(node_count)]
    bary_weights = np.array([1.0 / np.prod(entries) for entries in others])
    derivative = np.zeros((node_count, node_count))
    for row_id in range(node_count):
        for col_id in range(node_count):
            if row_id != col_id:
                derivative[row_id, col_id] = bary_weights[col_id] / bary_weights[row_id] / (points[row_id] - points[col_id])
        derivative[row_id, row_id] = -np.sum(derivative[row_id])
    stiffness = derivative.T @ (weights[:, None] * derivative)
    return stiffness, weights


def interpolation(coarse_count, fine_count):
    coarse_points = gll_nodes(coarse_count)[0]
    fine_points = gll_nodes(fine_count)[0]
    matrix = np.ones((fine_count, coarse_count))
    for row_id in range(fine_count):
        for col_id in range(coarse_count):
            for other in range(coarse_count):
                if other != col_id:
                    matrix[row_id, col_id] *= (fine_points[row_id] - coarse_points[other]) / (coarse_points[col_id] - coarse_points[other])
    return matrix


def chebyshev_bounds(node_count):
    stiffness, weights = lagrange_tables(node_count)
    row_abs = np.abs(stiffness).sum(axis=1)
    diag_vals = diagonal_of(stiffness)
    wide_one = weights[:, None, None]
    wide_two = weights[None, :, None]
    wide_three = weights[None, None, :]
    numerator = row_abs[:, None, None] * wide_two * wide_three + wide_one * row_abs[None, :, None] * wide_three + wide_one * wide_two * row_abs[None, None, :]
    denominator = diag_vals[:, None, None] * wide_two * wide_three + wide_one * diag_vals[None, :, None] * wide_three + wide_one * wide_two * diag_vals[None, None, :]
    top_bound = float(np.max(numerator / denominator))
    return top_bound, 0.1 * top_bound


def tiled(vector, length, position):
    repeated = jnp.asarray(np.tile(vector, length // vector.shape[0]), jnp.float32)
    return repeated.reshape(tuple(length if axis_id == position else 1 for axis_id in range(3)))


def along_first(values, matrix):
    out_count, in_count = matrix.shape
    blocks = values.shape[0] // in_count
    shaped = values.reshape(blocks, in_count, values.shape[1] * values.shape[2])
    result = jnp.einsum("ip,xpr->xir", jnp.asarray(matrix, jnp.float32), shaped, precision=HIGHEST)
    return result.reshape(blocks * out_count, values.shape[1], values.shape[2])


def along_second(values, matrix):
    out_count, in_count = matrix.shape
    blocks = values.shape[1] // in_count
    shaped = values.reshape(values.shape[0], blocks, in_count, values.shape[2])
    result = jnp.einsum("jq,xyqc->xyjc", jnp.asarray(matrix, jnp.float32), shaped, precision=HIGHEST)
    return result.reshape(values.shape[0], blocks * out_count, values.shape[2])


def along_third(values, matrix):
    out_count, in_count = matrix.shape
    blocks = values.shape[2] // in_count
    shaped = values.reshape(values.shape[0], values.shape[1], blocks, in_count)
    result = jnp.einsum("kq,xyeq->xyek", jnp.asarray(matrix, jnp.float32), shaped, precision=HIGHEST)
    return result.reshape(values.shape[0], values.shape[1], blocks * out_count)


def pass_first(padded, node_count):
    position = np.arange(padded.shape[0] - 2) % node_count
    at_start = jnp.asarray(position == 0, jnp.float32)[:, None, None]
    at_end = jnp.asarray(position == node_count - 1, jnp.float32)[:, None, None]
    return padded[1:-1] + at_start * padded[:-2] + at_end * padded[2:]


def pass_second(padded, node_count):
    position = np.arange(padded.shape[1] - 2) % node_count
    at_start = jnp.asarray(position == 0, jnp.float32)[None, :, None]
    at_end = jnp.asarray(position == node_count - 1, jnp.float32)[None, :, None]
    return padded[:, 1:-1] + at_start * padded[:, :-2] + at_end * padded[:, 2:]


def pass_third(values, node_count):
    position = np.arange(values.shape[2]) % node_count
    at_start = jnp.asarray(position == 0, jnp.float32)[None, None, :]
    at_end = jnp.asarray(position == node_count - 1, jnp.float32)[None, None, :]
    earlier = jnp.pad(values[:, :, :-1], ((0, 0), (0, 0), (1, 0)))
    following = jnp.pad(values[:, :, 1:], ((0, 0), (0, 0), (0, 1)))
    return values + at_start * earlier + at_end * following


def assemble(values, node_count):
    padded = jnp.pad(pass_third(values, node_count), ((1, 1), (1, 1), (0, 0)))
    return pass_second(pass_first(padded, node_count), node_count)


def spread_counts(elem_pad, node_count):
    position = np.arange(node_count)
    at_start = jnp.asarray(position == 0, jnp.float32)
    at_end = jnp.asarray(position == node_count - 1, jnp.float32)
    step_one = elem_pad[1:-1][:, None] + at_start[None, :, None, None] * elem_pad[:-2][:, None] + at_end[None, :, None, None] * elem_pad[2:][:, None]
    step_one = step_one.reshape(-1, elem_pad.shape[1], elem_pad.shape[2])
    step_two = step_one[:, 1:-1][:, :, None] + at_start[None, None, :, None] * step_one[:, :-2][:, :, None] + at_end[None, None, :, None] * step_one[:, 2:][:, :, None]
    step_two = step_two.reshape(step_one.shape[0], -1, elem_pad.shape[2])
    step_three = step_two[:, :, 1:-1][:, :, :, None] + at_start * step_two[:, :, :-2][:, :, :, None] + at_end * step_two[:, :, 2:][:, :, :, None]
    return step_three.reshape(step_two.shape[0], step_two.shape[1], -1)


def level_data(fluid_pad, exist_pad, node_count):
    fluid_count = spread_counts(fluid_pad, node_count)
    exist_count = spread_counts(exist_pad, node_count)
    ground = jnp.asarray(np.arange(fluid_count.shape[2]) > 0, jnp.float32)[None, None, :]
    node_mask = (fluid_count == exist_count).astype(jnp.float32) * (fluid_count > 0.5).astype(jnp.float32) * ground
    node_weight = 1.0 / exist_count
    fluid_cells = fluid_pad[1:-1, 1:-1, 1:-1]
    fluid_node = jnp.repeat(jnp.repeat(jnp.repeat(fluid_cells, node_count, axis=0), node_count, axis=1), node_count, axis=2)
    stiffness, weights = lagrange_tables(node_count)
    stiff_diag = diagonal_of(stiffness)
    dims_now = fluid_count.shape
    local_diag = tiled(stiff_diag, dims_now[0], 0) * tiled(weights, dims_now[1], 1) * tiled(weights, dims_now[2], 2)
    local_diag = local_diag + tiled(weights, dims_now[0], 0) * tiled(stiff_diag, dims_now[1], 1) * tiled(weights, dims_now[2], 2)
    local_diag = local_diag + tiled(weights, dims_now[0], 0) * tiled(weights, dims_now[1], 1) * tiled(stiff_diag, dims_now[2], 2)
    inverse_diag = node_mask / (fluid_count * local_diag + 1.0 - node_mask)
    return (node_count, fluid_node, node_mask, node_weight, inverse_diag)


def element_action(values, level_info):
    node_count, fluid_node = level_info[0], level_info[1]
    stiffness, weights = lagrange_tables(node_count)
    mass_first = tiled(weights, values.shape[0], 0)
    mass_second = tiled(weights, values.shape[1], 1)
    mass_third = tiled(weights, values.shape[2], 2)
    summed_terms = mass_second * mass_third * along_first(values, stiffness)
    summed_terms = summed_terms + mass_first * mass_third * along_second(values, stiffness)
    summed_terms = summed_terms + mass_first * mass_second * along_third(values, stiffness)
    return fluid_node * summed_terms


def apply_operator(values, level_info, assembler):
    return level_info[2] * assembler(element_action(values, level_info), level_info[0])


def smooth(target, start, level_info, bounds, assembler, from_zero):
    top_bound, low_bound = bounds
    center = 0.5 * (top_bound + low_bound)
    half_width = 0.5 * (top_bound - low_bound)
    inverse_diag = level_info[4]
    if from_zero:
        residual_now = target
        update = inverse_diag * residual_now / center
        solution = update
    else:
        residual_now = target - apply_operator(start, level_info, assembler)
        update = inverse_diag * residual_now / center
        solution = start + update
    residual_now = residual_now - apply_operator(update, level_info, assembler)
    rho_first = half_width / center
    rho_next = 1.0 / (2.0 * center / half_width - rho_first)
    update = rho_next * rho_first * update + (2.0 * rho_next / half_width) * inverse_diag * residual_now
    return solution + update


def restrict(values, coarse_count, fine_count):
    matrix = interpolation(coarse_count, fine_count).T
    return along_third(along_second(along_first(values, matrix), matrix), matrix)


def prolong(values, coarse_count, fine_count):
    matrix = interpolation(coarse_count, fine_count)
    return along_third(along_second(along_first(values, matrix), matrix), matrix)


def conjugate_gradients(target, level_info):
    node_weight = level_info[3]
    solution = jnp.zeros_like(target)
    residual_now = target
    direction = target
    norm_now = jnp.sum(node_weight * residual_now * residual_now)
    for iteration in range(CG_ITERS):
        applied = apply_operator(direction, level_info, assemble)
        step_len = norm_now / jnp.sum(node_weight * direction * applied)
        solution = solution + step_len * direction
        residual_now = residual_now - step_len * applied
        norm_next = jnp.sum(node_weight * residual_now * residual_now)
        direction = residual_now + (norm_next / norm_now) * direction
        norm_now = norm_next
    return solution


def vcycle(source, fluid_pad, exist_pad):
    fine_level = level_data(fluid_pad, exist_pad, 6)
    middle_level = level_data(fluid_pad, exist_pad, 4)
    coarse_level = level_data(fluid_pad, exist_pad, 2)
    fine_bounds = chebyshev_bounds(6)
    middle_bounds = chebyshev_bounds(4)
    target_fine = fine_level[2] * assemble(source, 6)
    fine_sol = smooth(target_fine, None, fine_level, fine_bounds, assemble, True)
    fine_res = target_fine - apply_operator(fine_sol, fine_level, assemble)
    target_middle = middle_level[2] * assemble(restrict(fine_level[3] * fine_res, 4, 6), 4)
    middle_sol = smooth(target_middle, None, middle_level, middle_bounds, assemble, True)
    middle_res = target_middle - apply_operator(middle_sol, middle_level, assemble)
    target_coarse = coarse_level[2] * assemble(restrict(middle_level[3] * middle_res, 2, 4), 2)
    coarse_sol = conjugate_gradients(target_coarse, coarse_level)
    middle_sol = middle_sol + middle_level[2] * prolong(coarse_sol, 2, 4)
    middle_sol = smooth(target_middle, middle_sol, middle_level, middle_bounds, assemble, False)
    fine_sol = fine_sol + fine_level[2] * prolong(middle_sol, 4, 6)
    fine_sol = smooth(target_fine, fine_sol, fine_level, fine_bounds, assemble, False)
    return fine_sol, coarse_sol


def reference(pressure_source, building_heights):
    column = pressure_source.shape[2] // 6
    heights_pad = jnp.pad(building_heights, 1, constant_values=column)
    exist_cols = jnp.pad(jnp.ones(building_heights.shape, jnp.float32), 1)
    layers = jnp.arange(-1, column + 1, dtype=jnp.int32)
    inside = ((layers >= 0) & (layers < column)).astype(jnp.float32)[None, None, :]
    fluid_pad = (layers[None, None, :] >= heights_pad[:, :, None]).astype(jnp.float32) * inside
    exist_pad = exist_cols[:, :, None] * inside
    correction, coarse_solution = vcycle(pressure_source, fluid_pad, exist_pad)
    return (correction, coarse_solution)
```

```python
import functools

import jax
import jax.numpy as jnp
import numpy as np
from jax import lax
from jax.experimental import pallas as pl
from jax.experimental.pallas import tpu as pltpu
from jax.sharding import PartitionSpec as P

CG_ITERS = 10
VMEM = pl.BlockSpec(memory_space=pltpu.VMEM)
SMEM = pl.BlockSpec(memory_space=pltpu.SMEM)
F32 = jnp.float32


def gll_nodes(n):
    if n == 6:
        o, m = 0.7650553239294647, 0.2852315164806451
        points = [-1.0, -o, -m, m, o, 1.0]
        w = [1.0 / 15.0, 0.378474956297847, 0.5548583770354863]
        weights = w + w[::-1]
    elif n == 4:
        m = 0.4472135954999579
        points = [-1.0, -m, m, 1.0]
        weights = [1.0 / 6.0, 5.0 / 6.0, 5.0 / 6.0, 1.0 / 6.0]
    else:
        points, weights = [-1.0, 1.0], [1.0, 1.0]
    return np.array(points), np.array(weights)


def lagrange_tables(n):
    points, weights = gll_nodes(n)
    bary = np.array(
        [1.0 / np.prod([points[c] - points[o] for o in range(n) if o != c]) for c in range(n)]
    )
    deriv = np.zeros((n, n))
    for r in range(n):
        for c in range(n):
            if r != c:
                deriv[r, c] = bary[c] / bary[r] / (points[r] - points[c])
        deriv[r, r] = -np.sum(deriv[r])
    return deriv.T @ (weights[:, None] * deriv), weights


def interpolation(coarse, fine):
    xc, xf = gll_nodes(coarse)[0], gll_nodes(fine)[0]
    m = np.ones((fine, coarse))
    for r in range(fine):
        for c in range(coarse):
            for o in range(coarse):
                if o != c:
                    m[r, c] *= (xf[r] - xc[o]) / (xc[c] - xc[o])
    return m


def diag_table(n):
    s, w = lagrange_tables(n)
    d = np.diag(s)
    return (
        d[:, None, None] * w[None, :, None] * w[None, None, :]
        + w[:, None, None] * d[None, :, None] * w[None, None, :]
        + w[:, None, None] * w[None, :, None] * d[None, None, :]
    )


def cheb(n):
    s, w = lagrange_tables(n)
    r = np.abs(s).sum(axis=1)
    num = (
        r[:, None, None] * w[None, :, None] * w[None, None, :]
        + w[:, None, None] * r[None, :, None] * w[None, None, :]
        + w[:, None, None] * w[None, :, None] * r[None, None, :]
    )
    top = float(np.max(num / diag_table(n)))
    center, half = 0.5 * (top + 0.1 * top), 0.5 * (top - 0.1 * top)
    rho0 = half / center
    rho1 = 1.0 / (2.0 * center / half - rho0)
    return center, rho1 * rho0, 2.0 * rho1 / half


def lane_iota(rows=8):
    return lax.broadcasted_iota(jnp.int32, (rows, 128), 1)


def row_iota(rows=8):
    return lax.broadcasted_iota(jnp.int32, (rows, 128), 0)


def per(n):
    return n * n * (n // 2)


def ix(n, i, j, k):
    return (i * n + j) * (n // 2) + k


def at(slot, rows):
    start = slot * rows
    if not isinstance(start, int):
        start = pl.multiple_of(start, 8)
    return pl.ds(start, rows)


def ld(ref, slot, rows):
    return ref[at(slot, rows), :]


def st(ref, slot, rows, value):
    ref[at(slot, rows), :] = value


def swap(v):
    return pltpu.roll(v, 64, 1)


def cs_apply(m, v):
    no, ni = m.shape
    h = ni // 2
    e = [v[q] + v[ni - 1 - q] for q in range(h)]
    o = [v[q] - v[ni - 1 - q] for q in range(h)]
    out = [None] * no
    for p in range(no // 2):
        a = b = None
        for q in range(h):
            ce = float(0.5 * (m[p, q] + m[p, ni - 1 - q]))
            co = float(0.5 * (m[p, q] - m[p, ni - 1 - q]))
            ta, tb = e[q] * ce, o[q] * co
            a = ta if a is None else a + ta
            b = tb if b is None else b + tb
        out[p], out[no - 1 - p] = a + b, a - b
    return out


def cs_fold(m, v):
    no, ni = m.shape
    r = [swap(x) for x in v]
    out = []
    for p in range(no // 2):
        a = None
        for q in range(ni // 2):
            t = v[q] * float(m[p, q]) + r[q] * float(m[p, ni - 1 - q])
            a = t if a is None else a + t
        out.append(a)
    return out


def k_slab(n, src, a_src, acc, rows, emit):
    s, w = lagrange_tables(n)
    sh = s / w[:, None]
    kh, cnt = n // 2, per(n)
    base = a_src * cnt
    for j in range(n):
        for k in range(kh):
            line = cs_apply(sh, [ld(src, base + ix(n, i, j, k), rows) for i in range(n)])
            for i in range(n):
                st(acc, ix(n, i, j, k), rows, line[i])
    for i in range(n):
        v = [[ld(src, base + ix(n, i, j, k), rows) for k in range(kh)] for j in range(n)]
        t = [cs_fold(sh, v[j]) for j in range(n)]
        for k in range(kh):
            line = cs_apply(sh, [v[j][k] for j in range(n)])
            for j in range(n):
                total = t[j][k] + line[j] + ld(acc, ix(n, i, j, k), rows)
                t[j][k] = total * float(w[i] * w[j] * w[k])
        emit(i, t)


def z_partner(v):
    lane = lane_iota(v.shape[0])
    moved = jnp.where(lane < 64, pltpu.roll(v, 65, 1), pltpu.roll(v, 63, 1))
    return jnp.where((lane == 0) | (lane == 127), 0.0, moved)


def zy_sum(n, t):
    for j in range(n):
        t[j][0] = t[j][0] + z_partner(t[j][0])
    rows = t[0][0].shape[0]
    for k in range(n // 2):
        a, b = t[0][k], t[n - 1][k]
        t[0][k] = a + pltpu.roll(b, 1, 0)
        t[n - 1][k] = b + pltpu.roll(a, rows - 1, 0)
    return t


def put_plane(n, ref, base, i, t, rows):
    for j in range(n):
        for k in range(n // 2):
            st(ref, base + ix(n, i, j, k), rows, t[j][k])


def x_summed(n, ref, a, i, j, k, rows, low=True, high=True):
    cnt = per(n)
    v = ld(ref, a * cnt + ix(n, i, j, k), rows)
    if i == 0 and low is not False:
        v = v + ld(ref, (a - 1) * cnt + ix(n, n - 1, j, k), rows)
    if i == n - 1 and high is not False:
        v = v + ld(ref, (a + 1) * cnt + ix(n, 0, j, k), rows)
    return v


def cls(n, i):
    return 0 if i == 0 else (2 if i == n - 1 else 1)


def gslot(n, a, i, j, k):
    return ((a * 3 + cls(n, i)) * 3 + cls(n, j)) * 2 + (0 if k == 0 else 1)


def nodes(n):
    return [(i, j, k) for i in range(n) for j in range(n) for k in range(n // 2)]


def own_rows():
    row = row_iota()
    return (row >= 2) & (row < 6)


def own_sum(n, t_ref, out_ref):
    def body(a, carry):
        for i, j, k in nodes(n):
            st(out_ref, a * per(n) + ix(n, i, j, k), 8, x_summed(n, t_ref, a + 1, i, j, k, 8))
        return carry

    lax.fori_loop(0, 4, body, 0)


def zero_face(n, ref, a, i, rows):
    for j in range(n):
        for k in range(n // 2):
            st(ref, a * per(n) + ix(n, i, j, k), rows, jnp.zeros((rows, 128), F32))


def pack_column(n, src, a, dst, slot0):
    row = row_iota()
    cnt = per(n)
    for m in range(cnt // 2):
        u = ld(src, a * cnt + 2 * m, 8)
        v = ld(src, a * cnt + 2 * m + 1, 8)
        st(dst, slot0 + m, 8, jnp.where(row < 4, pltpu.roll(u, 6, 0), pltpu.roll(v, 2, 0)))


def own_row_lines(n, src, dst_lo, dst_hi):
    cnt = per(n)
    for a in range(4):
        dst_lo[pl.ds(a * cnt, cnt), :] = src[pl.ds(a * cnt * 8 + 2, cnt, stride=8), :]
        dst_hi[pl.ds(a * cnt, cnt), :] = src[pl.ds(a * cnt * 8 + 5, cnt, stride=8), :]


def split3(x):
    hi = x.astype(jnp.bfloat16)
    rest = x - hi.astype(F32)
    mid = rest.astype(jnp.bfloat16)
    return hi, mid, (rest - mid.astype(F32)).astype(jnp.bfloat16)


def exact_dot(x, perm):
    hi, mid, lo = split3(x)
    dot = functools.partial(jnp.dot, preferred_element_type=F32)
    return dot(hi, perm) + dot(mid, perm) + dot(lo, perm)


def layout_kernel(src_ref, perm_ref, s_ref, b_ref, ml_ref, mr_ref, lo_ref, hi_ref, y_ref, t_ref):
    y = exact_dot(src_ref[...], perm_ref[...])
    for k in range(3):
        y_ref[pl.ds(624 * k, 16), :] = jnp.zeros((16, 128), F32)
        y_ref[pl.ds(624 * k + 592, 32), :] = jnp.zeros((32, 128), F32)
        y_ref[pl.ds(624 * k + 16, 576), :] = y[:, 128 * k : 128 * k + 128]
    own = own_rows()
    n, cnt = 6, per(6)
    zero_face(n, t_ref, 0, n - 1, 8)
    zero_face(n, t_ref, 5, 0, 8)
    for a in range(4):
        for i in range(n):
            t = [[None] * 3 for _ in range(n)]
            for j in range(n):
                start = 16 + (a * 6 + i) * 24 + j - 12
                for k in range(3):
                    v = y_ref[pl.ds(624 * k + start, 8, stride=6), :]
                    v = jnp.where(own, v, 0.0)
                    st(s_ref, a * cnt + ix(n, i, j, k), 8, v)
                    t[j][k] = v
            put_plane(n, t_ref, (a + 1) * cnt, i, zy_sum(n, t), 8)
    own_sum(n, t_ref, b_ref)
    pack_column(n, b_ref, 0, ml_ref, 0)
    pack_column(n, b_ref, 3, mr_ref, 0)
    own_row_lines(n, b_ref, lo_ref, hi_ref)


def flags(ids_ref):
    gx, gy = ids_ref[0], ids_ref[1]
    one = lambda c: jnp.where(c, 1.0, 0.0).astype(F32)
    return one(gx > 0), one(gx < ids_ref[2] - 1), one(gy > 0), one(gy < ids_ref[3] - 1)


def y_line(n, h, own_line, fl, fr, left, right, b, dst, off, partial):
    cnt = per(n)
    q = cnt // n
    for t in range(h):
        dst[pl.ds(off + t * cnt, cnt), :] = fl * left[pl.ds(t * cnt * 4 + b, cnt, stride=4), :]
        dst[pl.ds(off + (4 + h + t) * cnt, cnt), :] = (
            fr * right[pl.ds(t * cnt * 4 + b, cnt, stride=4), :]
        )
    for a in range(4):
        dst[pl.ds(off + (h + a) * cnt, cnt), :] = own_line(a)
    if partial:
        for edge in (h, h + 4):
            lo = pl.ds(off + edge * cnt - q, q)
            hi = pl.ds(off + edge * cnt, q)
            total = dst[lo, :] + dst[hi, :]
            dst[lo, :] = total
            dst[hi, :] = total


def y_lines_kernel(n, ids_ref, lo_ref, hi_ref, left_ref, right_ref, dn_ref, up_ref):
    fl, fr, _, _ = flags(ids_ref)
    cnt = per(n)
    for b, src, dst in ((0, lo_ref, dn_ref), (3, hi_ref, up_ref)):
        line = lambda a, src=src: src[pl.ds(a * cnt, cnt), :]
        y_line(n, 1, line, fl, fr, left_ref, right_ref, b, dst, 0, True)


def unpack(n, h, a0, rows, r0, own, left, right, low, high, offs, fl, dst, partial):
    fleft, fright, flow, fhigh = fl
    oleft, olow = offs
    cnt = per(n)
    row = row_iota()
    keep = own_rows()
    shift = r0 - 2

    def place(v):
        v = jnp.where(keep, v, 0.0)
        if shift:
            v = pltpu.roll(v, shift, 0)
        if rows > 8:
            v = jnp.concatenate([v, jnp.zeros((rows - 8, 128), F32)], axis=0)
        return v

    def own_body(a, carry):
        for m in range(cnt):
            st(dst, (a0 + a) * cnt + m, rows, place(ld(own, a * cnt + m, 8)))
        return carry

    lax.fori_loop(0, 4, own_body, 0)
    for src, f, first in ((left, fleft, a0 - h), (right, fright, a0 + 4)):

        def ring_body(t, carry, src=src, f=f, first=first):
            for m in range(cnt // 2):
                v = f * ld(src, oleft // 8 + t * (cnt // 2) + m, 8)
                st(dst, (first + t) * cnt + 2 * m, rows, place(pltpu.roll(v, 2, 0)))
                st(dst, (first + t) * cnt + 2 * m + 1, rows, place(pltpu.roll(v, 6, 0)))
            return carry

        lax.fori_loop(0, h, ring_body, 0)
    if partial:
        for edge in (a0, a0 + 4):
            for j in range(n):
                for k in range(n // 2):
                    lo = (edge - 1) * cnt + ix(n, n - 1, j, k)
                    hi = edge * cnt + ix(n, 0, j, k)
                    total = ld(dst, lo, rows) + ld(dst, hi, rows)
                    st(dst, lo, rows, total)
                    st(dst, hi, rows, total)
    wide = 4 + 2 * h
    for src, f, first in ((low, flow, r0 - h), (high, fhigh, r0 + 4)):
        for t in range(h):
            for a in range(wide):
                line = f * src[pl.ds(olow + (t * wide + a) * cnt, cnt), :]
                dst[pl.ds((a0 - h + a) * cnt * rows + first + t, cnt, stride=rows), :] = line
    if partial:
        row = row_iota(rows)
        to_hi = (row == r0) | (row == r0 + 4)
        to_lo = (row == r0 - 1) | (row == r0 + 3)

        def y_body(a, carry):
            for i in range(n):
                for k in range(n // 2):
                    lo = (a0 - h + a) * cnt + ix(n, i, 0, k)
                    hi = (a0 - h + a) * cnt + ix(n, i, n - 1, k)
                    u, v = ld(dst, lo, rows), ld(dst, hi, rows)
                    st(dst, lo, rows, u + jnp.where(to_hi, pltpu.roll(v, 1, 0), 0.0))
                    st(dst, hi, rows, v + jnp.where(to_lo, pltpu.roll(u, rows - 1, 0), 0.0))
            return carry

        lax.fori_loop(0, wide, y_body, 0)


def down_smooth(n, b_ref, g_ref, g0, u_ref, t_ref, acc_ref, z_ref):
    center, ca, cb = cheb(n)
    d = diag_table(n)
    cnt = per(n)
    own = own_rows()

    def first(a, carry):
        for i, j, k in nodes(n):
            s = a * cnt + ix(n, i, j, k)
            g = ld(g_ref, gslot(n, a + g0, i, j, k), 8)
            st(u_ref, s, 8, g * ld(b_ref, s, 8) * float(1.0 / (d[i, j, k] * center)))
        return carry

    lax.fori_loop(0, 6, first, 0)

    def second(a, carry):
        put = lambda i, t: put_plane(n, t_ref, a * cnt, i, zy_sum(n, t), 8)
        k_slab(n, u_ref, a, acc_ref, 8, put)
        return carry

    lax.fori_loop(0, 6, second, 0)

    def third(a, carry):
        for i, j, k in nodes(n):
            s = (a + 1) * cnt + ix(n, i, j, k)
            g = ld(g_ref, gslot(n, a + 1 + g0, i, j, k), 8)
            r = ld(b_ref, s, 8) - x_summed(n, t_ref, a + 1, i, j, k, 8)
            z = ld(u_ref, s, 8) * (1.0 + ca) + g * r * float(cb / d[i, j, k])
            st(z_ref, a * cnt + ix(n, i, j, k), 8, jnp.where(own, z, 0.0))
        return carry

    lax.fori_loop(0, 4, third, 0)


def down_residual(n, nc, s_ref, z_ref, g_ref, g0, t_ref, acc_ref, w1_ref, w2_ref, rp_ref, emit):
    cnt = per(n)
    kh, kc = n // 2, nc // 2
    m = interpolation(nc, n).T
    zero_face(n, t_ref, 0, n - 1, 8)
    zero_face(n, t_ref, 5, 0, 8)

    def body(a, carry):
        def put(i, t):
            for j in range(n):
                for k in range(kh):
                    t[j][k] = ld(s_ref, a * cnt + ix(n, i, j, k), 8) - t[j][k]
                    g = ld(g_ref, gslot(n, a + 1 + g0, i, j, k), 8)
                    st(w1_ref, ix(n, i, j, k), 8, jnp.where(g > 0.0, t[j][k], 0.0))
            put_plane(n, t_ref, (a + 1) * cnt, i, zy_sum(n, t), 8)

        k_slab(n, z_ref, a, acc_ref, 8, put)
        for j in range(n):
            for k in range(kh):
                line = cs_apply(m, [ld(w1_ref, ix(n, i, j, k), 8) for i in range(n)])
                for i in range(nc):
                    st(w2_ref, ix(n, i, j, k), 8, line[i])
        coarse = []
        for i in range(nc):
            cols = []
            for k in range(kh):
                cols.append(cs_apply(m, [ld(w2_ref, ix(n, i, j, k), 8) for j in range(n)]))
            plane = [cs_fold(m, [cols[k][j] for k in range(kh)]) for j in range(nc)]
            emit(a, i, plane)
        return carry

    lax.fori_loop(0, 4, body, 0)
    own_sum(n, t_ref, rp_ref)


def fine_down_kernel(
    ids_ref, s_ref, bp_ref, left_ref, right_ref, low_ref, high_ref, g_ref,
    z_ref, rp_ref, ml_ref, mr_ref, s3_ref, b3_ref, m3l_ref, m3r_ref, lo3_ref, hi3_ref,
    b_ref, u_ref, t_ref, acc_ref, w1_ref, w2_ref, t3_ref,
):
    fl = flags(ids_ref)
    unpack(6, 1, 1, 8, 2, bp_ref, left_ref, right_ref, low_ref, high_ref, (0, 0), fl, b_ref, True)
    down_smooth(6, b_ref, g_ref, 1, u_ref, t_ref, acc_ref, z_ref)
    c3 = per(4)
    zero_face(4, t3_ref, 0, 3, 8)
    zero_face(4, t3_ref, 5, 0, 8)

    def emit(a, i, plane):
        put_plane(4, s3_ref, a * c3, i, plane, 8)
        put_plane(4, t3_ref, (a + 1) * c3, i, zy_sum(4, plane), 8)

    down_residual(
        6, 4, s_ref, z_ref, g_ref, 1, t_ref, acc_ref, w1_ref, w2_ref, rp_ref, emit
    )
    own_sum(4, t3_ref, b3_ref)
    pack_column(4, b3_ref, 0, m3l_ref, 0)
    pack_column(4, b3_ref, 3, m3r_ref, 0)
    own_row_lines(4, b3_ref, lo3_ref, hi3_ref)
    pack_column(6, rp_ref, 0, ml_ref, 0)
    pack_column(6, rp_ref, 3, mr_ref, 0)


X5, X3R, X3Z = 108 * 4, 3 * 32 * 4, 2 * 32 * 4
Y5, Y3R, Y3Z = 6 * 108, 3 * 10 * 32, 2 * 8 * 32


def middle_down_kernel(
    ids_ref, s_ref, bp_ref, left_ref, right_ref, low_ref, high_ref, g_ref, m5l_ref, m5r_ref,
    z_ref, rp_ref, ml_ref, mr_ref, block_ref,
    b_ref, u_ref, t_ref, acc_ref, w1_ref, w2_ref, c_ref,
):
    fl = flags(ids_ref)
    unpack(4, 1, 1, 8, 2, bp_ref, left_ref, right_ref, low_ref, high_ref, (0, 0), fl, b_ref, True)
    down_smooth(4, b_ref, g_ref, 1, u_ref, t_ref, acc_ref, z_ref)

    def emit(a, i, plane):
        lane = lane_iota()
        line = []
        for j in range(2):
            v = plane[j][0]
            line.append(swap(v) + jnp.where(lane < 63, pltpu.roll(v, 127, 1), 0.0))
        st(c_ref, a * 2 + i, 8, line[0] + pltpu.roll(line[1], 1, 0))

    down_residual(
        4, 2, s_ref, z_ref, g_ref, 1, t_ref, acc_ref, w1_ref, w2_ref, rp_ref, emit
    )
    planes = []
    for a in range(5):
        v = None
        if a < 4:
            v = ld(c_ref, a * 2, 8)
        if a > 0:
            u = ld(c_ref, (a - 1) * 2 + 1, 8)
            v = u if v is None else v + u
        planes.append(v)
    lane = lane_iota()
    block_ref[...] = jnp.zeros((16, 128), F32)
    for p in range(3):
        v = planes[2 * p]
        other = swap(planes[2 * p + 1]) if p < 2 else jnp.zeros((8, 128), F32)
        v = jnp.where(lane < 64, v, other)
        block_ref[pl.ds(5 * p, 5), :] = v[2:7]
    ml_ref[pl.ds(0, X5), :] = m5l_ref[...]
    mr_ref[pl.ds(0, X5), :] = m5r_ref[...]
    for t in range(3):
        pack_column(4, rp_ref, t, ml_ref, X5 // 8 + t * 16)
        pack_column(4, rp_ref, 1 + t, mr_ref, X5 // 8 + t * 16)
    for t in range(2):
        pack_column(4, z_ref, t, ml_ref, (X5 + X3R) // 8 + t * 16)
        pack_column(4, z_ref, 2 + t, mr_ref, (X5 + X3R) // 8 + t * 16)


def up_lines_kernel(ids_ref, r5_ref, r3_ref, z3_ref, left_ref, right_ref, dn_ref, up_ref):
    fl, fr, _, _ = flags(ids_ref)
    for dst, r5row, r3rows, z3rows in (
        (dn_ref, 0, (0, 1, 2), (0, 1)),
        (up_ref, 3, (1, 2, 3), (2, 3)),
    ):
        def line(src, cnt, b):
            return lambda a: src[pl.ds(a * cnt * 8 + 2 + b, cnt, stride=8), :]

        def part(ref, start, size):
            return ref.at[pl.ds(start, size), :]

        y_line(
            6, 1, line(r5_ref, 108, r5row), fl, fr, part(left_ref, 0, X5), part(right_ref, 0, X5),
            r5row, dst, 0, True,
        )
        for t, b in enumerate(r3rows):
            y_line(
                4, 3, line(r3_ref, 32, b), fl, fr, part(left_ref, X5, X3R),
                part(right_ref, X5, X3R), b, dst, Y5 + t * 320, True,
            )
        for t, b in enumerate(z3rows):
            y_line(
                4, 2, line(z3_ref, 32, b), fl, fr, part(left_ref, X5 + X3R, X3Z),
                part(right_ref, X5 + X3R, X3Z), b, dst, Y5 + Y3R + t * 256, False,
            )


def coarse_kernel(
    ids_ref, gath_ref, w_ref, perm_ref, win_ref, out_ref, x_ref, r_ref, p_ref, q_ref, o_ref
):
    gy = ids_ref[1]
    gx = ids_ref[0]
    lane = lane_iota(72)
    body = pl.ds(8, 72)
    for ref in (x_ref, r_ref, p_ref, q_ref):
        ref[...] = jnp.zeros(ref.shape, F32)
    lane16 = lane_iota(16)
    for g in range(4):
        for i in range(5):
            for r in range(5):
                lo = gath_ref[pl.ds((g * 16) * 16 + (i // 2) * 5 + r, 16, stride=16), :]
                hi = gath_ref[
                    pl.ds(((7 - g) * 16) * 16 + ((4 - i) // 2) * 5 + r, 16, stride=16), :
                ]
                if i % 2 == 0:
                    v = jnp.where(lane16 < 64, lo, swap(hi))
                else:
                    v = jnp.where(lane16 < 64, swap(lo), hi)
                rows = pl.ds(8 + r, 16, stride=4)
                r_ref[4 * g + i, rows, :] = r_ref[4 * g + i, rows, :] + v
    mid = r_ref[16, body, :]
    r_ref[16, body, :] = mid + swap(mid)

    def fold(v):
        return jnp.sum(v.reshape(9, 8, 128), axis=0)

    acc = jnp.zeros((8, 128), F32)
    for la in range(17):
        v = jnp.where(w_ref[la] > 0.0, r_ref[la, body, :], 0.0)
        r_ref[la, body, :] = v
        acc = acc + fold(v * v) * (0.5 if la == 16 else 1.0)
    rr = jnp.sum(acc)

    kk = lane & 63
    zdn = jnp.where(kk == 0, 0.0, jnp.where(kk == 63, 1.0, 0.5)).astype(F32)
    zup = jnp.where(kk == 63, 0.0, 0.5).astype(F32)
    brow = row_iota(72)
    yco = jnp.where((brow == 0) | (brow == 64), 1.0, 0.5).astype(F32)

    def iterate(_, carry):
        rr, beta = carry
        for la in range(17):
            p_ref[la, body, :] = r_ref[la, body, :] + beta * p_ref[la, body, :]
        acc = jnp.zeros((8, 128), F32)
        for la in range(17):
            v = p_ref[la, body, :]
            if la == 0:
                xs = p_ref[1, body, :]
            elif la == 16:
                u = p_ref[15, body, :]
                xs = 0.5 * (u + swap(u))
            else:
                xs = 0.5 * (p_ref[la - 1, body, :] + p_ref[la + 1, body, :])
            ys = yco * (p_ref[la, pl.ds(7, 72), :] + p_ref[la, pl.ds(9, 72), :])
            zs = zdn * pltpu.roll(v, 1, 1) + zup * pltpu.roll(v, 127, 1)
            q = w_ref[la] * (3.0 * v - xs - ys - zs)
            q_ref[la, body, :] = q
            acc = acc + fold(v * q) * (0.5 if la == 16 else 1.0)
        step = rr / jnp.sum(acc)
        acc = jnp.zeros((8, 128), F32)
        for la in range(17):
            x_ref[la, body, :] = x_ref[la, body, :] + step * p_ref[la, body, :]
            v = r_ref[la, body, :] - step * q_ref[la, body, :]
            r_ref[la, body, :] = v
            acc = acc + fold(v * v) * (0.5 if la == 16 else 1.0)
        new = jnp.sum(acc)
        return new, new / rr

    lax.fori_loop(0, CG_ITERS, iterate, (rr, jnp.zeros((), F32)))

    lane24 = lane_iota(24)
    row0 = pl.multiple_of(4 + 4 * gy, 4)
    for t in range(13):
        a = jnp.clip(4 * gx - 4 + t, 0, 32)
        v = x_ref[jnp.minimum(a, 32 - a), pl.ds(row0, 24), :]
        v = jnp.where(a > 16, swap(v), v)
        bottom = jnp.where(lane24 == 0, 0.0, pltpu.roll(v, 1, 1))
        win_ref[t] = jnp.where(lane24 < 64, bottom, swap(v))
    for a in range(4):
        for i in range(2):
            for j in range(2):
                o_ref[pl.ds((2 * a + i) * 8 + j, 4, stride=2), :] = win_ref[
                    4 + a + i, pl.ds(4 + j, 4), :
                ]
    out_ref[...] = exact_dot(o_ref[...], perm_ref[...])


def up_smooth(n, wide, rows, v_ref, r_ref, g_ref, u_ref, t_ref, acc_ref, finish):
    center, ca, cb = cheb(n)
    d = diag_table(n)
    cnt = per(n)

    def apply_to(src, lo, hi):
        def body(a, carry):
            put = lambda i, t: put_plane(n, t_ref, a * cnt, i, zy_sum(n, t), rows)
            k_slab(n, src, a, acc_ref, rows, put)
            return carry

        lax.fori_loop(lo, hi, body, 0)

    apply_to(v_ref, 0, wide)

    def first(a, carry):
        for i, j, k in nodes(n):
            s = a * cnt + ix(n, i, j, k)
            r = ld(r_ref, s, rows) - x_summed(n, t_ref, a, i, j, k, rows)
            st(r_ref, s, rows, r)
            g = ld(g_ref, gslot(n, a, i, j, k), rows)
            st(u_ref, s, rows, g * r * float(1.0 / (d[i, j, k] * center)))
        return carry

    lax.fori_loop(1, wide - 1, first, 0)
    apply_to(u_ref, 1, wide - 1)

    def second(a, carry):
        for i, j, k in nodes(n):
            s = a * cnt + ix(n, i, j, k)
            r = ld(r_ref, s, rows) - x_summed(n, t_ref, a, i, j, k, rows)
            g = ld(g_ref, gslot(n, a, i, j, k), rows)
            x = ld(v_ref, s, rows) + ld(u_ref, s, rows) * (1.0 + ca)
            finish(a, i, j, k, x + g * r * float(cb / d[i, j, k]))
        return carry

    lax.fori_loop(2, wide - 2, second, 0)


def up_kernel(
    ids_ref, win_ref, r5p_ref, z5_ref, r3p_ref, z3p_ref, left_ref, right_ref, low_ref, high_ref,
    g5_ref, g3_ref, perm_ref, out_ref,
    v3_ref, r3_ref, z3_ref, u3_ref, t3_ref, a3_ref, v5_ref, r5_ref, u5_ref, t5_ref, a5_ref,
    w1_ref, w2_ref, y_ref,
):
    fl = flags(ids_ref)
    c3, c5 = per(4), per(6)

    def take(n, h, a0, rows, r0, own, offs, dst, partial):
        unpack(
            n, h, a0, rows, r0, own, left_ref, right_ref, low_ref, high_ref, offs, fl, dst, partial
        )

    take(6, 1, 2, 8, 2, r5p_ref, (0, 0), r5_ref, True)
    take(4, 3, 4, 16, 4, r3p_ref, (X5, Y5), r3_ref, True)
    take(4, 2, 4, 16, 4, z3p_ref, (X5 + X3R, Y5 + Y3R), z3_ref, False)

    m = interpolation(2, 4)

    def prolong1(a, carry):
        corner = [[[win_ref[a + i, pl.ds(j, 16), :]] for j in range(2)] for i in range(2)]
        along = [cs_apply(m, [corner[0][j][0], corner[1][j][0]]) for j in range(2)]
        for i in range(4):
            line = cs_apply(m, [along[0][i], along[1][i]])
            for j in range(4):
                v = cs_fold(m, [line[j]])
                for k in range(2):
                    g = ld(g3_ref, gslot(4, a, i, j, k), 16)
                    st(v3_ref, a * c3 + ix(4, i, j, k), 16, jnp.where(g > 0.0, v[k], 0.0))
        return carry

    lax.fori_loop(0, 12, prolong1, 0)

    def finish3(a, i, j, k, x):
        s = a * c3 + ix(4, i, j, k)
        st(z3_ref, s, 16, ld(z3_ref, s, 16) + x)

    up_smooth(4, 12, 16, v3_ref, r3_ref, g3_ref, u3_ref, t3_ref, a3_ref, finish3)

    m5 = interpolation(4, 6)

    def prolong3(a, carry):
        for j in range(4):
            for k in range(2):
                src = []
                for i in range(4):
                    v = ld(z3_ref, (a + 2) * c3 + ix(4, i, j, k), 16)
                    src.append(v[2:10])
                line = cs_apply(m5, src)
                for i in range(6):
                    st(w1_ref, (i * 4 + j) * 2 + k, 8, line[i])
        for i in range(6):
            cols = []
            for k in range(2):
                cols.append(cs_apply(m5, [ld(w1_ref, (i * 4 + j) * 2 + k, 8) for j in range(4)]))
            for j in range(6):
                v = cs_fold(m5, [cols[k][j] for k in range(2)])
                for k in range(3):
                    g = ld(g5_ref, gslot(6, a, i, j, k), 8)
                    st(v5_ref, a * c5 + ix(6, i, j, k), 8, jnp.where(g > 0.0, v[k], 0.0))
        return carry

    lax.fori_loop(0, 8, prolong3, 0)

    def finish5(a, i, j, k, x):
        s = ix(6, i, j, k)
        v = ld(z5_ref, (a - 2) * c5 + s, 8) + x
        start = ((a - 2) * 6 + i) * 24 + j
        y_ref[pl.ds(576 * k + start, 4, stride=6), :] = v[2:6]

    up_smooth(6, 8, 8, v5_ref, r5_ref, g5_ref, u5_ref, t5_ref, a5_ref, finish5)
    y = jnp.concatenate([y_ref[pl.ds(576 * k, 576), :] for k in range(3)], axis=1)
    out_ref[...] = exact_dot(y, perm_ref[...])


def class_maps(heights, gx, gy, ring, rows, r0):
    na, nb = heights.shape
    w = 4 + 2 * ring + 2
    pad = ((ring + 1, ring + 1), (ring + 1, ring + 1))
    start = (4 * gx, 4 * gy)
    h = lax.dynamic_slice(jnp.pad(heights, pad), start, (w, w))
    e = lax.dynamic_slice(jnp.pad(jnp.ones((na, nb), F32), pad), start, (w, w))
    ax = jnp.arange(w) + 4 * gx - ring - 1
    ay = jnp.arange(w) + 4 * gy - ring - 1
    fx = ((ax >= 0) & (ax < na)).astype(F32)
    fy = ((ay >= 0) & (ay < nb)).astype(F32)
    hx = jnp.stack([jnp.maximum(h[:-2], h[1:-1]), h[1:-1], jnp.maximum(h[1:-1], h[2:])], 1)
    hxy = jnp.stack(
        [
            jnp.maximum(hx[:, :, :-2], hx[:, :, 1:-1]),
            hx[:, :, 1:-1],
            jnp.maximum(hx[:, :, 1:-1], hx[:, :, 2:]),
        ],
        2,
    )
    own = e[1:-1, 1:-1][:, None, None, :]
    hxy = jnp.where(own > 0.0, hxy, 1000)

    def inv(f):
        return jnp.stack([1.0 / (1.0 + f[:-2]), jnp.ones_like(f[1:-1]), 1.0 / (1.0 + f[2:])], 1)

    exy = inv(fx)[:, :, None, None] * inv(fy).T[None, None, :, :]
    extra = rows - (w - 2)
    hxy = jnp.pad(hxy, ((0, 0), (0, 0), (0, 0), (0, extra)), constant_values=1000)
    exy = jnp.pad(exy, ((0, 0), (0, 0), (0, 0), (0, extra)))
    lane = jnp.arange(128)
    c = lane & 63
    bound = jnp.stack([jnp.where(lane < 64, c - 1, c), c])
    zfac = jnp.stack([jnp.where(lane == 127, 1.0, 0.5), jnp.ones(128)]).astype(F32)
    g = jnp.where(
        bound[None, None, None, :, None, :] >= hxy[:, :, :, None, :, None],
        exy[:, :, :, None, :, None] * zfac[None, None, None, :, None, :],
        0.0,
    )
    return g.reshape(-1, 128)


def coarse_weight(heights):
    na, nb = heights.shape
    h = jnp.pad(heights, 1)
    hn = jnp.maximum(h[:-1], h[1:])
    hn = jnp.maximum(hn[:, :-1], hn[:, 1:])
    half = na // 2
    hn = jnp.stack([hn[: half + 1], hn[half:][::-1]], 2)
    hn = jnp.pad(hn, ((0, 0), (0, 72 - nb - 1), (0, 0)), constant_values=1000)
    hn = jnp.repeat(hn, 64, axis=2)
    la = jnp.arange(half + 1)
    b = jnp.arange(72)
    kk = jnp.arange(128) & 63
    ex = jnp.where(la == 0, 1.0, 2.0)[:, None, None]
    ey = jnp.where((b == 0) | (b == nb), 1.0, 2.0)[None, :, None]
    ez = jnp.where(kk == 63, 1.0, 2.0)[None, None, :]
    return jnp.where(kk[None, None, :] >= hn, 0.5 * ex * ey * ez, 0.0).astype(F32)


def perm_in():
    m = np.zeros((384, 384), np.float32)
    for z in range(384):
        c, k = divmod(z, 6)
        m[z, k * 128 + c if k < 3 else (5 - k) * 128 + 64 + c] = 1.0
    return m


def perm_coarse():
    m = np.zeros((128, 128), np.float32)
    for c in range(64):
        m[c, 2 * c] = 1.0
        m[64 + c, 2 * c + 1] = 1.0
    return m


def call(kernel, outs, ins, scratch):
    return pl.pallas_call(
        kernel,
        out_shape=[jax.ShapeDtypeStruct(s, F32) for s in outs],
        in_specs=ins,
        out_specs=[VMEM] * len(outs),
        scratch_shapes=[pltpu.VMEM(s, F32) for s in scratch],
        compiler_params=pltpu.CompilerParams(vmem_limit_bytes=56 * 1024 * 1024),
    )


def both_ways(axis, to_low, to_high):
    n = lax.axis_size(axis)
    from_low = lax.ppermute(to_high, axis, [(i, (i + 1) % n) for i in range(n)])
    from_high = lax.ppermute(to_low, axis, [(i, (i - 1) % n) for i in range(n)])
    return from_low, from_high


def per_device(source, heights):
    gx, gy = lax.axis_index("gx"), lax.axis_index("gy")
    nx, ny = lax.axis_size("gx"), lax.axis_size("gy")
    ids = jnp.stack([gx, gy, nx, ny]).astype(jnp.int32)
    g5 = class_maps(heights, gx, gy, 2, 8, 2)
    g3d = class_maps(heights, gx, gy, 2, 8, 2)
    g3 = class_maps(heights, gx, gy, 4, 16, 4)
    cw = coarse_weight(heights)
    pin = jnp.asarray(perm_in(), jnp.bfloat16)
    pout = jnp.asarray(perm_in().T, jnp.bfloat16)
    pc = jnp.asarray(perm_coarse(), jnp.bfloat16)

    def f(n, a):
        return (a * per(n) * 8, 128)

    s5, b5p, ml, mr, lo, hi = call(
        layout_kernel,
        [f(6, 4), f(6, 4), (432, 128), (432, 128), (432, 128), (432, 128)],
        [VMEM] * 2,
        [(1872, 128), f(6, 6)],
    )(source.reshape(576, 384), pin)
    left, right = both_ways("gx", ml, mr)
    dn, up = call(
        functools.partial(y_lines_kernel, 6), [(648, 128)] * 2, [SMEM] + [VMEM] * 4, []
    )(ids, lo, hi, left, right)
    low, high = both_ways("gy", dn, up)
    z5, r5p, m5l, m5r, s3, b3p, ml, mr, lo, hi = call(
        fine_down_kernel,
        [f(6, 4), f(6, 4), (432, 128), (432, 128), f(4, 4), f(4, 4)] + [(128, 128)] * 4,
        [SMEM] + [VMEM] * 7,
        [f(6, 6), f(6, 6), f(6, 6), f(6, 1), f(6, 1), f(6, 1), f(4, 6)],
    )(ids, s5, b5p, left, right, low, high, g5)
    left, right = both_ways("gx", ml, mr)
    dn, up = call(
        functools.partial(y_lines_kernel, 4), [(192, 128)] * 2, [SMEM] + [VMEM] * 4, []
    )(ids, lo, hi, left, right)
    low, high = both_ways("gy", dn, up)
    xr, yr = X5 + X3R + X3Z, Y5 + Y3R + Y3Z
    z3, r3p, ml, mr, block = call(
        middle_down_kernel,
        [f(4, 4), f(4, 4), (xr, 128), (xr, 128), (16, 128)],
        [SMEM] + [VMEM] * 9,
        [f(4, 6), f(4, 6), f(4, 6), f(4, 1), f(4, 1), f(4, 1), (64, 128)],
    )(ids, s3, b3p, left, right, low, high, g3d, m5l, m5r)
    every = jnp.broadcast_to(block[None], (nx * ny, 16, 128))
    gath = lax.all_to_all(every, ("gx", "gy"), 0, 0).reshape(nx * ny * 16, 128)
    left, right = both_ways("gx", ml, mr)
    dn, up = call(up_lines_kernel, [(yr, 128)] * 2, [SMEM] + [VMEM] * 5, [])(
        ids, r5p, r3p, z3, left, right
    )
    low, high = both_ways("gy", dn, up)
    win, coarse = call(
        coarse_kernel,
        [(13, 24, 128), (64, 128)],
        [SMEM] + [VMEM] * 3,
        [(17, 88, 128)] * 4 + [(64, 128)],
    )(ids, gath, cw, pc)

    def f16(a):
        return (a * per(4) * 16, 128)

    (out,) = call(
        up_kernel,
        [(576, 384)],
        [SMEM] + [VMEM] * 12,
        [f16(12), f16(12), f16(12), f16(12), f16(12), f16(1)]
        + [f(6, 8), f(6, 8), f(6, 8), f(6, 8), f(6, 1), f(6, 1), f(6, 1), (1728, 128)],
    )(ids, win, r5p, z5, r3p, z3, left, right, low, high, g5, g3, pout)
    return out.reshape(24, 24, 384), coarse.reshape(8, 8, 128)


def solution(mesh):
    spec = P("gx", "gy", None)
    return jax.shard_map(
        per_device, mesh=mesh, in_specs=(spec, P()), out_specs=(spec, spec), check_vma=False
    )
```

```python
import functools

import jax
import jax.numpy as jnp
import numpy as np
from jax import lax
from jax.experimental import pallas as pl
from jax.experimental.pallas import tpu as pltpu
from jax.sharding import PartitionSpec as P

CG_ITERS = 10
VMEM = pl.BlockSpec(memory_space=pltpu.VMEM)
ANY = pl.BlockSpec(memory_space=pl.ANY)
SMEM = pl.BlockSpec(memory_space=pltpu.SMEM)
F32 = jnp.float32


def gll_nodes(n):
    if n == 6:
        o, m = 0.7650553239294647, 0.2852315164806451
        points = [-1.0, -o, -m, m, o, 1.0]
        w = [1.0 / 15.0, 0.378474956297847, 0.5548583770354863]
        weights = w + w[::-1]
    elif n == 4:
        m = 0.4472135954999579
        points = [-1.0, -m, m, 1.0]
        weights = [1.0 / 6.0, 5.0 / 6.0, 5.0 / 6.0, 1.0 / 6.0]
    else:
        points, weights = [-1.0, 1.0], [1.0, 1.0]
    return np.array(points), np.array(weights)


def lagrange_tables(n):
    points, weights = gll_nodes(n)
    bary = np.array(
        [1.0 / np.prod([points[c] - points[o] for o in range(n) if o != c]) for c in range(n)]
    )
    deriv = np.zeros((n, n))
    for r in range(n):
        for c in range(n):
            if r != c:
                deriv[r, c] = bary[c] / bary[r] / (points[r] - points[c])
        deriv[r, r] = -np.sum(deriv[r])
    return deriv.T @ (weights[:, None] * deriv), weights


def interpolation(coarse, fine):
    xc, xf = gll_nodes(coarse)[0], gll_nodes(fine)[0]
    m = np.ones((fine, coarse))
    for r in range(fine):
        for c in range(coarse):
            for o in range(coarse):
                if o != c:
                    m[r, c] *= (xf[r] - xc[o]) / (xc[c] - xc[o])
    return m


def diag_table(n):
    s, w = lagrange_tables(n)
    d = np.diag(s)
    return (
        d[:, None, None] * w[None, :, None] * w[None, None, :]
        + w[:, None, None] * d[None, :, None] * w[None, None, :]
        + w[:, None, None] * w[None, :, None] * d[None, None, :]
    )


def cheb(n):
    s, w = lagrange_tables(n)
    r = np.abs(s).sum(axis=1)
    num = (
        r[:, None, None] * w[None, :, None] * w[None, None, :]
        + w[:, None, None] * r[None, :, None] * w[None, None, :]
        + w[:, None, None] * w[None, :, None] * r[None, None, :]
    )
    top = float(np.max(num / diag_table(n)))
    center, half = 0.5 * (top + 0.1 * top), 0.5 * (top - 0.1 * top)
    rho0 = half / center
    rho1 = 1.0 / (2.0 * center / half - rho0)
    return center, rho1 * rho0, 2.0 * rho1 / half


def lane_iota(rows=8):
    return lax.broadcasted_iota(jnp.int32, (rows, 128), 1)


def row_iota(rows=8):
    return lax.broadcasted_iota(jnp.int32, (rows, 128), 0)


def per(n):
    return n * n * (n // 2)


def ix(n, i, j, k):
    return (i * n + j) * (n // 2) + k


def at(slot, rows):
    start = slot * rows
    if not isinstance(start, int):
        start = pl.multiple_of(start, 8)
    return pl.ds(start, rows)


def ld(ref, slot, rows):
    return ref[at(slot, rows), :]


def st(ref, slot, rows, value):
    ref[at(slot, rows), :] = value


def swap(v):
    return pltpu.roll(v, 64, 1)


def cs_apply(m, v):
    no, ni = m.shape
    h = ni // 2
    e = [v[q] + v[ni - 1 - q] for q in range(h)]
    o = [v[q] - v[ni - 1 - q] for q in range(h)]
    out = [None] * no
    for p in range(no // 2):
        a = b = None
        for q in range(h):
            ce = float(0.5 * (m[p, q] + m[p, ni - 1 - q]))
            co = float(0.5 * (m[p, q] - m[p, ni - 1 - q]))
            ta, tb = e[q] * ce, o[q] * co
            a = ta if a is None else a + ta
            b = tb if b is None else b + tb
        out[p], out[no - 1 - p] = a + b, a - b
    return out


def cs_fold(m, v):
    no, ni = m.shape
    r = [swap(x) for x in v]
    out = []
    for p in range(no // 2):
        a = None
        for q in range(ni // 2):
            t = v[q] * float(m[p, q]) + r[q] * float(m[p, ni - 1 - q])
            a = t if a is None else a + t
        out.append(a)
    return out


def k_slab(n, src, a_src, acc, rows, emit):
    s, w = lagrange_tables(n)
    sh = s / w[:, None]
    kh, cnt = n // 2, per(n)
    base = a_src * cnt
    for j in range(n):
        for k in range(kh):
            line = cs_apply(sh, [ld(src, base + ix(n, i, j, k), rows) for i in range(n)])
            for i in range(n):
                st(acc, ix(n, i, j, k), rows, line[i])
    for i in range(n):
        v = [[ld(src, base + ix(n, i, j, k), rows) for k in range(kh)] for j in range(n)]
        t = [cs_fold(sh, v[j]) for j in range(n)]
        for k in range(kh):
            line = cs_apply(sh, [v[j][k] for j in range(n)])
            for j in range(n):
                total = t[j][k] + line[j] + ld(acc, ix(n, i, j, k), rows)
                t[j][k] = total * float(w[i] * w[j] * w[k])
        emit(i, t)


def k_face(n, src, a_src, i, rows, emit):
    s, w = lagrange_tables(n)
    sh = s / w[:, None]
    kh, cnt = n // 2, per(n)
    base = a_src * cnt
    v = [[ld(src, base + ix(n, i, j, k), rows) for k in range(kh)] for j in range(n)]
    t = [cs_fold(sh, v[j]) for j in range(n)]
    for k in range(kh):
        line = cs_apply(sh, [v[j][k] for j in range(n)])
        for j in range(n):
            total = t[j][k] + line[j]
            for q in range(n):
                x = v[j][k] if q == i else ld(src, base + ix(n, q, j, k), rows)
                total = total + x * float(sh[i, q])
            t[j][k] = total * float(w[i] * w[j] * w[k])
    emit(i, t)


def z_partner(v):
    lane = lane_iota(v.shape[0])
    moved = jnp.where(lane < 64, pltpu.roll(v, 65, 1), pltpu.roll(v, 63, 1))
    return jnp.where((lane == 0) | (lane == 127), 0.0, moved)


def zy_sum(n, t):
    for j in range(n):
        t[j][0] = t[j][0] + z_partner(t[j][0])
    rows = t[0][0].shape[0]
    for k in range(n // 2):
        a, b = t[0][k], t[n - 1][k]
        t[0][k] = a + pltpu.roll(b, 1, 0)
        t[n - 1][k] = b + pltpu.roll(a, rows - 1, 0)
    return t


def put_plane(n, ref, base, i, t, rows):
    for j in range(n):
        for k in range(n // 2):
            st(ref, base + ix(n, i, j, k), rows, t[j][k])


def apply_columns(n, src, t_ref, acc_ref, lo, hi, rows):
    def put(a):
        return lambda i, t: put_plane(n, t_ref, a * per(n), i, zy_sum(n, t), rows)

    k_face(n, src, lo, n - 1, rows, put(lo))
    k_face(n, src, hi - 1, 0, rows, put(hi - 1))

    def body(a, carry):
        k_slab(n, src, a, acc_ref, rows, put(a))
        return carry

    lax.fori_loop(lo + 1, hi - 1, body, 0)


def x_summed(n, ref, a, i, j, k, rows, low=True, high=True):
    cnt = per(n)
    v = ld(ref, a * cnt + ix(n, i, j, k), rows)
    if i == 0 and low is not False:
        v = v + ld(ref, (a - 1) * cnt + ix(n, n - 1, j, k), rows)
    if i == n - 1 and high is not False:
        v = v + ld(ref, (a + 1) * cnt + ix(n, 0, j, k), rows)
    return v


def cls(n, i):
    return 0 if i == 0 else (2 if i == n - 1 else 1)


def gslot(n, a, i, j, k):
    return ((a * 3 + cls(n, i)) * 3 + cls(n, j)) * 2 + (0 if k == 0 else 1)


def nodes(n):
    return [(i, j, k) for i in range(n) for j in range(n) for k in range(n // 2)]


def own_rows():
    row = row_iota()
    return (row >= 2) & (row < 6)


def own_sum(n, t_ref, out_ref):
    def body(a, carry):
        for i, j, k in nodes(n):
            st(out_ref, a * per(n) + ix(n, i, j, k), 8, x_summed(n, t_ref, a + 1, i, j, k, 8))
        return carry

    lax.fori_loop(0, 4, body, 0)


def zero_face(n, ref, a, i, rows):
    for j in range(n):
        for k in range(n // 2):
            st(ref, a * per(n) + ix(n, i, j, k), rows, jnp.zeros((rows, 128), F32))


def pack_column(n, src, a, dst, slot0):
    row = row_iota()
    cnt = per(n)
    for m in range(cnt // 2):
        u = ld(src, a * cnt + 2 * m, 8)
        v = ld(src, a * cnt + 2 * m + 1, 8)
        st(dst, slot0 + m, 8, jnp.where(row < 4, pltpu.roll(u, 6, 0), pltpu.roll(v, 2, 0)))


def own_row_lines(n, src, dst_lo, dst_hi):
    cnt = per(n)
    for a in range(4):
        dst_lo[pl.ds(a * cnt, cnt), :] = src[pl.ds(a * cnt * 8 + 2, cnt, stride=8), :]
        dst_hi[pl.ds(a * cnt, cnt), :] = src[pl.ds(a * cnt * 8 + 5, cnt, stride=8), :]


def split3(x):
    hi = x.astype(jnp.bfloat16)
    rest = x - hi.astype(F32)
    mid = rest.astype(jnp.bfloat16)
    return hi, mid, (rest - mid.astype(F32)).astype(jnp.bfloat16)


def exact_dot(x, perm):
    hi, mid, lo = split3(x)
    dot = functools.partial(jnp.dot, preferred_element_type=F32)
    return dot(hi, perm) + dot(mid, perm) + dot(lo, perm)


def layout_kernel(src_ref, perm_ref, s_ref, b_ref, ml_ref, mr_ref, lo_ref, hi_ref, y_ref, t_ref):
    y = exact_dot(src_ref[...], perm_ref[...])
    for k in range(3):
        y_ref[pl.ds(624 * k, 16), :] = jnp.zeros((16, 128), F32)
        y_ref[pl.ds(624 * k + 592, 32), :] = jnp.zeros((32, 128), F32)
        y_ref[pl.ds(624 * k + 16, 576), :] = y[:, 128 * k : 128 * k + 128]
    own = own_rows()
    n, cnt = 6, per(6)
    zero_face(n, t_ref, 0, n - 1, 8)
    zero_face(n, t_ref, 5, 0, 8)
    for a in range(4):
        for i in range(n):
            t = [[None] * 3 for _ in range(n)]
            for j in range(n):
                start = 16 + (a * 6 + i) * 24 + j - 12
                for k in range(3):
                    v = y_ref[pl.ds(624 * k + start, 8, stride=6), :]
                    v = jnp.where(own, v, 0.0)
                    st(s_ref, a * cnt + ix(n, i, j, k), 8, v)
                    t[j][k] = v
            put_plane(n, t_ref, (a + 1) * cnt, i, zy_sum(n, t), 8)
    own_sum(n, t_ref, b_ref)
    pack_column(n, b_ref, 0, ml_ref, 0)
    pack_column(n, b_ref, 3, mr_ref, 0)
    own_row_lines(n, b_ref, lo_ref, hi_ref)


def flags(ids_ref):
    gx, gy = ids_ref[0], ids_ref[1]
    one = lambda c: jnp.where(c, 1.0, 0.0).astype(F32)
    return one(gx > 0), one(gx < ids_ref[2] - 1), one(gy > 0), one(gy < ids_ref[3] - 1)


def y_line(n, h, own_line, fl, fr, left, right, b, dst, off, partial):
    cnt = per(n)
    q = cnt // n
    for t in range(h):
        dst[pl.ds(off + t * cnt, cnt), :] = fl * left[pl.ds(t * cnt * 4 + b, cnt, stride=4), :]
        dst[pl.ds(off + (4 + h + t) * cnt, cnt), :] = (
            fr * right[pl.ds(t * cnt * 4 + b, cnt, stride=4), :]
        )
    for a in range(4):
        dst[pl.ds(off + (h + a) * cnt, cnt), :] = own_line(a)
    if partial:
        for edge in (h, h + 4):
            lo = pl.ds(off + edge * cnt - q, q)
            hi = pl.ds(off + edge * cnt, q)
            total = dst[lo, :] + dst[hi, :]
            dst[lo, :] = total
            dst[hi, :] = total


def y_lines_kernel(n, ids_ref, lo_ref, hi_ref, left_ref, right_ref, dn_ref, up_ref):
    fl, fr, _, _ = flags(ids_ref)
    cnt = per(n)
    for b, src, dst in ((0, lo_ref, dn_ref), (3, hi_ref, up_ref)):
        line = lambda a, src=src: src[pl.ds(a * cnt, cnt), :]
        y_line(n, 1, line, fl, fr, left_ref, right_ref, b, dst, 0, True)


def unpack(n, h, a0, rows, r0, own, left, right, low, high, offs, fl, dst, partial):
    fleft, fright, flow, fhigh = fl
    oleft, olow = offs
    cnt = per(n)
    row = row_iota()
    keep = own_rows()
    shift = r0 - 2

    def place(v):
        v = jnp.where(keep, v, 0.0)
        if shift:
            v = pltpu.roll(v, shift, 0)
        if rows > 8:
            v = jnp.concatenate([v, jnp.zeros((rows - 8, 128), F32)], axis=0)
        return v

    def own_body(a, carry):
        for m in range(cnt):
            st(dst, (a0 + a) * cnt + m, rows, place(ld(own, a * cnt + m, 8)))
        return carry

    lax.fori_loop(0, 4, own_body, 0)
    for src, f, first in ((left, fleft, a0 - h), (right, fright, a0 + 4)):

        def ring_body(t, carry, src=src, f=f, first=first):
            for m in range(cnt // 2):
                v = f * ld(src, oleft // 8 + t * (cnt // 2) + m, 8)
                st(dst, (first + t) * cnt + 2 * m, rows, place(pltpu.roll(v, 2, 0)))
                st(dst, (first + t) * cnt + 2 * m + 1, rows, place(pltpu.roll(v, 6, 0)))
            return carry

        lax.fori_loop(0, h, ring_body, 0)
    if partial:
        for edge in (a0, a0 + 4):
            for j in range(n):
                for k in range(n // 2):
                    lo = (edge - 1) * cnt + ix(n, n - 1, j, k)
                    hi = edge * cnt + ix(n, 0, j, k)
                    total = ld(dst, lo, rows) + ld(dst, hi, rows)
                    st(dst, lo, rows, total)
                    st(dst, hi, rows, total)
    wide = 4 + 2 * h
    for src, f, first in ((low, flow, r0 - h), (high, fhigh, r0 + 4)):
        for t in range(h):
            for a in range(wide):
                line = f * src[pl.ds(olow + (t * wide + a) * cnt, cnt), :]
                dst[pl.ds((a0 - h + a) * cnt * rows + first + t, cnt, stride=rows), :] = line
    if partial:
        row = row_iota(rows)
        to_hi = (row == r0) | (row == r0 + 4)
        to_lo = (row == r0 - 1) | (row == r0 + 3)

        def y_body(a, carry):
            for i in range(n):
                for k in range(n // 2):
                    lo = (a0 - h + a) * cnt + ix(n, i, 0, k)
                    hi = (a0 - h + a) * cnt + ix(n, i, n - 1, k)
                    u, v = ld(dst, lo, rows), ld(dst, hi, rows)
                    st(dst, lo, rows, u + jnp.where(to_hi, pltpu.roll(v, 1, 0), 0.0))
                    st(dst, hi, rows, v + jnp.where(to_lo, pltpu.roll(u, rows - 1, 0), 0.0))
            return carry

        lax.fori_loop(0, wide, y_body, 0)


def down_smooth(n, b_ref, g_ref, g0, u_ref, t_ref, acc_ref, z_ref):
    center, ca, cb = cheb(n)
    d = diag_table(n)
    cnt = per(n)
    own = own_rows()

    def first(a, carry):
        for i, j, k in nodes(n):
            s = a * cnt + ix(n, i, j, k)
            g = ld(g_ref, gslot(n, a + g0, i, j, k), 8)
            st(u_ref, s, 8, g * ld(b_ref, s, 8) * float(1.0 / (d[i, j, k] * center)))
        return carry

    lax.fori_loop(0, 6, first, 0)

    apply_columns(n, u_ref, t_ref, acc_ref, 0, 6, 8)

    def third(a, carry):
        for i, j, k in nodes(n):
            s = (a + 1) * cnt + ix(n, i, j, k)
            g = ld(g_ref, gslot(n, a + 1 + g0, i, j, k), 8)
            r = ld(b_ref, s, 8) - x_summed(n, t_ref, a + 1, i, j, k, 8)
            z = ld(u_ref, s, 8) * (1.0 + ca) + g * r * float(cb / d[i, j, k])
            st(z_ref, a * cnt + ix(n, i, j, k), 8, jnp.where(own, z, 0.0))
        return carry

    lax.fori_loop(0, 4, third, 0)


def down_residual(n, nc, s_ref, z_ref, g_ref, g0, t_ref, acc_ref, w1_ref, w2_ref, rp_ref, emit):
    cnt = per(n)
    kh, kc = n // 2, nc // 2
    m = interpolation(nc, n).T
    zero_face(n, t_ref, 0, n - 1, 8)
    zero_face(n, t_ref, 5, 0, 8)

    def body(a, carry):
        def put(i, t):
            for j in range(n):
                for k in range(kh):
                    t[j][k] = ld(s_ref, a * cnt + ix(n, i, j, k), 8) - t[j][k]
                    g = ld(g_ref, gslot(n, a + 1 + g0, i, j, k), 8)
                    st(w1_ref, ix(n, i, j, k), 8, jnp.where(g > 0.0, t[j][k], 0.0))
            put_plane(n, t_ref, (a + 1) * cnt, i, zy_sum(n, t), 8)

        k_slab(n, z_ref, a, acc_ref, 8, put)
        for j in range(n):
            for k in range(kh):
                line = cs_apply(m, [ld(w1_ref, ix(n, i, j, k), 8) for i in range(n)])
                for i in range(nc):
                    st(w2_ref, ix(n, i, j, k), 8, line[i])
        coarse = []
        for i in range(nc):
            cols = []
            for k in range(kh):
                cols.append(cs_apply(m, [ld(w2_ref, ix(n, i, j, k), 8) for j in range(n)]))
            plane = [cs_fold(m, [cols[k][j] for k in range(kh)]) for j in range(nc)]
            emit(a, i, plane)
        return carry

    lax.fori_loop(0, 4, body, 0)
    own_sum(n, t_ref, rp_ref)


def fine_down_kernel(
    ids_ref, s_in, bp_ref, left_ref, right_ref, low_ref, high_ref, g_ref,
    z_out, rp_ref, ml_ref, mr_ref, lo_ref, hi_ref, s3_ref, b3_ref, m3l_ref, m3r_ref, lo3_ref, hi3_ref,
    b_ref, u_ref, t_ref, acc_ref, w1_ref, w2_ref, t3_ref, s_ref, z_ref, sem,
):
    fl = flags(ids_ref)
    get_s = pltpu.make_async_copy(s_in, s_ref, sem.at[0])
    put_z = pltpu.make_async_copy(z_ref, z_out, sem.at[1])
    get_s.start()
    unpack(6, 1, 1, 8, 2, bp_ref, left_ref, right_ref, low_ref, high_ref, (0, 0), fl, b_ref, True)
    down_smooth(6, b_ref, g_ref, 1, u_ref, t_ref, acc_ref, z_ref)
    put_z.start()
    get_s.wait()
    c3 = per(4)
    zero_face(4, t3_ref, 0, 3, 8)
    zero_face(4, t3_ref, 5, 0, 8)

    def emit(a, i, plane):
        put_plane(4, s3_ref, a * c3, i, plane, 8)
        put_plane(4, t3_ref, (a + 1) * c3, i, zy_sum(4, plane), 8)

    down_residual(
        6, 4, s_ref, z_ref, g_ref, 1, t_ref, acc_ref, w1_ref, w2_ref, rp_ref, emit
    )
    own_sum(4, t3_ref, b3_ref)
    pack_column(4, b3_ref, 0, m3l_ref, 0)
    pack_column(4, b3_ref, 3, m3r_ref, 0)
    own_row_lines(4, b3_ref, lo3_ref, hi3_ref)
    pack_column(6, rp_ref, 0, ml_ref, 0)
    pack_column(6, rp_ref, 3, mr_ref, 0)
    own_row_lines(6, rp_ref, lo_ref, hi_ref)
    put_z.wait()


X3R, X3Z = 3 * 32 * 4, 2 * 32 * 4
Y3R, Y3Z = 3 * 10 * 32, 2 * 8 * 32


def middle_down_kernel(
    ids_ref, s_ref, bp_ref, left_ref, right_ref, low_ref, high_ref, g_ref,
    z_ref, rp_ref, block_ref, ml_ref, mr_ref,
    b_ref, u_ref, t_ref, acc_ref, w1_ref, w2_ref, c_ref,
):
    fl = flags(ids_ref)
    unpack(4, 1, 1, 8, 2, bp_ref, left_ref, right_ref, low_ref, high_ref, (0, 0), fl, b_ref, True)
    down_smooth(4, b_ref, g_ref, 1, u_ref, t_ref, acc_ref, z_ref)

    def emit(a, i, plane):
        lane = lane_iota()
        line = []
        for j in range(2):
            v = plane[j][0]
            line.append(swap(v) + jnp.where(lane < 63, pltpu.roll(v, 127, 1), 0.0))
        st(c_ref, a * 2 + i, 8, line[0] + pltpu.roll(line[1], 1, 0))

    down_residual(
        4, 2, s_ref, z_ref, g_ref, 1, t_ref, acc_ref, w1_ref, w2_ref, rp_ref, emit
    )
    planes = []
    for a in range(5):
        v = None
        if a < 4:
            v = ld(c_ref, a * 2, 8)
        if a > 0:
            u = ld(c_ref, (a - 1) * 2 + 1, 8)
            v = u if v is None else v + u
        planes.append(v)
    lane = lane_iota()
    blank = jnp.zeros((1, 128), F32)
    rows = []
    for p in range(3):
        v = planes[2 * p]
        other = swap(planes[2 * p + 1]) if p < 2 else jnp.zeros((8, 128), F32)
        v = jnp.where(lane < 64, v, other)
        rows.append(v[2:7])
    block = jnp.concatenate(rows + [blank], axis=0)
    for d in range(block_ref.shape[0] // 16):
        block_ref[pl.ds(16 * d, 16), :] = block

    for t in range(3):
        pack_column(4, rp_ref, t, ml_ref, t * 16)
        pack_column(4, rp_ref, 1 + t, mr_ref, t * 16)
    for t in range(2):
        pack_column(4, z_ref, t, ml_ref, X3R // 8 + t * 16)
        pack_column(4, z_ref, 2 + t, mr_ref, X3R // 8 + t * 16)


def up_lines_kernel(ids_ref, r3_ref, z3_ref, left_ref, right_ref, dn_ref, up_ref):
    fl, fr, _, _ = flags(ids_ref)
    for dst, r3rows, z3rows in (
        (dn_ref, (0, 1, 2), (0, 1)),
        (up_ref, (1, 2, 3), (2, 3)),
    ):
        def line(src, cnt, b):
            return lambda a: src[pl.ds(a * cnt * 8 + 2 + b, cnt, stride=8), :]

        def part(ref, start, size):
            return ref.at[pl.ds(start, size), :]

        for t, b in enumerate(r3rows):
            y_line(
                4, 3, line(r3_ref, 32, b), fl, fr, part(left_ref, 0, X3R),
                part(right_ref, 0, X3R), b, dst, t * 320, True,
            )
        for t, b in enumerate(z3rows):
            y_line(
                4, 2, line(z3_ref, 32, b), fl, fr, part(left_ref, X3R, X3Z),
                part(right_ref, X3R, X3Z), b, dst, Y3R + t * 256, False,
            )


def coarse_kernel(
    ids_ref, same_ref, other_ref, w_ref, perm_ref, win_ref, out_ref, x_ref, r_ref, p_ref, q_ref, o_ref
):
    gy = ids_ref[1]
    gx = ids_ref[0]
    lane = lane_iota(72)
    body = pl.ds(8, 72)
    for ref in (x_ref, r_ref, p_ref, q_ref):
        ref[...] = jnp.zeros(ref.shape, F32)
    lane16 = lane_iota(16)
    even = lax.rem(gx, 2) == 0

    def lines(g, row):
        where = pl.ds((g // 2) * 256 + row, 16, stride=16)
        u, v = same_ref[where, :], other_ref[where, :]
        return jnp.where(even, u, v) if g % 2 == 0 else jnp.where(even, v, u)

    for g in range(4):
        for i in range(5):
            for r in range(5):
                lo = lines(g, (i // 2) * 5 + r)
                hi = lines(7 - g, ((4 - i) // 2) * 5 + r)
                if i % 2 == 0:
                    v = jnp.where(lane16 < 64, lo, swap(hi))
                else:
                    v = jnp.where(lane16 < 64, swap(lo), hi)
                rows = pl.ds(8 + r, 16, stride=4)
                r_ref[4 * g + i, rows, :] = r_ref[4 * g + i, rows, :] + v
    mid = r_ref[16, body, :]
    r_ref[16, body, :] = mid + swap(mid)

    def fold(v):
        return jnp.sum(v.reshape(9, 8, 128), axis=0)

    acc = jnp.zeros((8, 128), F32)
    for la in range(17):
        v = jnp.where(w_ref[la] > 0.0, r_ref[la, body, :], 0.0)
        r_ref[la, body, :] = v
        acc = acc + fold(v * v) * (0.5 if la == 16 else 1.0)
    rr = jnp.sum(acc)

    kk = lane & 63
    zdn = jnp.where(kk == 0, 0.0, jnp.where(kk == 63, 1.0, 0.5)).astype(F32)
    zup = jnp.where(kk == 63, 0.0, 0.5).astype(F32)
    brow = row_iota(72)
    yco = jnp.where((brow == 0) | (brow == 64), 1.0, 0.5).astype(F32)

    def iterate(_, carry):
        rr, beta = carry
        for la in range(17):
            p_ref[la, body, :] = r_ref[la, body, :] + beta * p_ref[la, body, :]
        acc = jnp.zeros((8, 128), F32)
        for la in range(17):
            v = p_ref[la, body, :]
            if la == 0:
                xs = p_ref[1, body, :]
            elif la == 16:
                u = p_ref[15, body, :]
                xs = 0.5 * (u + swap(u))
            else:
                xs = 0.5 * (p_ref[la - 1, body, :] + p_ref[la + 1, body, :])
            ys = yco * (p_ref[la, pl.ds(7, 72), :] + p_ref[la, pl.ds(9, 72), :])
            zs = zdn * pltpu.roll(v, 1, 1) + zup * pltpu.roll(v, 127, 1)
            q = w_ref[la] * (3.0 * v - xs - ys - zs)
            q_ref[la, body, :] = q
            acc = acc + fold(v * q) * (0.5 if la == 16 else 1.0)
        step = rr / jnp.sum(acc)
        acc = jnp.zeros((8, 128), F32)
        for la in range(17):
            x_ref[la, body, :] = x_ref[la, body, :] + step * p_ref[la, body, :]
            v = r_ref[la, body, :] - step * q_ref[la, body, :]
            r_ref[la, body, :] = v
            acc = acc + fold(v * v) * (0.5 if la == 16 else 1.0)
        new = jnp.sum(acc)
        return new, new / rr

    lax.fori_loop(0, CG_ITERS, iterate, (rr, jnp.zeros((), F32)))

    lane24 = lane_iota(24)
    row0 = pl.multiple_of(4 + 4 * gy, 4)
    for t in range(13):
        a = jnp.clip(4 * gx - 4 + t, 0, 32)
        v = x_ref[jnp.minimum(a, 32 - a), pl.ds(row0, 24), :]
        v = jnp.where(a > 16, swap(v), v)
        bottom = jnp.where(lane24 == 0, 0.0, pltpu.roll(v, 1, 1))
        win_ref[t] = jnp.where(lane24 < 64, bottom, swap(v))
    for a in range(4):
        for i in range(2):
            for j in range(2):
                o_ref[pl.ds((2 * a + i) * 8 + j, 4, stride=2), :] = win_ref[
                    4 + a + i, pl.ds(4 + j, 4), :
                ]
    out_ref[...] = exact_dot(o_ref[...], perm_ref[...])


def up_smooth(n, wide, rows, v_ref, r_ref, g_ref, u_ref, t_ref, acc_ref, before_residual, finish):
    center, ca, cb = cheb(n)
    d = diag_table(n)
    cnt = per(n)

    apply_columns(n, v_ref, t_ref, acc_ref, 0, wide, rows)
    before_residual()

    def first(a, carry):
        for i, j, k in nodes(n):
            s = a * cnt + ix(n, i, j, k)
            r = ld(r_ref, s, rows) - x_summed(n, t_ref, a, i, j, k, rows)
            st(r_ref, s, rows, r)
            g = ld(g_ref, gslot(n, a, i, j, k), rows)
            st(u_ref, s, rows, g * r * float(1.0 / (d[i, j, k] * center)))
        return carry

    lax.fori_loop(1, wide - 1, first, 0)
    apply_columns(n, u_ref, t_ref, acc_ref, 1, wide - 1, rows)

    def second(a, carry):
        for i, j, k in nodes(n):
            s = a * cnt + ix(n, i, j, k)
            r = ld(r_ref, s, rows) - x_summed(n, t_ref, a, i, j, k, rows)
            g = ld(g_ref, gslot(n, a, i, j, k), rows)
            x = ld(v_ref, s, rows) + ld(u_ref, s, rows) * (1.0 + ca)
            finish(a, i, j, k, x + g * r * float(cb / d[i, j, k]))
        return carry

    lax.fori_loop(2, wide - 2, second, 0)


def up_kernel(
    ids_ref, win_ref, r5p_in, z5_in, r3p_in, z3p_in, left_in, right_in, low_in, high_in,
    left5_in, right5_in, low5_in, high5_in,
    g5_in, g3_in, perm_ref, out_ref,
    r5p_ref, z5_ref, r3p_ref, z3p_ref, left_ref, right_ref, low_ref, high_ref,
    left5_ref, right5_ref, low5_ref, high5_ref, g5_ref, g3_ref, sem,
    v3_ref, r3_ref, z3_ref, u3_ref, t3_ref, a3_ref, v5_ref, r5_ref, u5_ref, t5_ref, a5_ref,
    w1_ref, w2_ref, y_ref,
):
    fl = flags(ids_ref)
    c3, c5 = per(4), per(6)
    moves = [
        (g3_in, g3_ref), (left_in, left_ref), (right_in, right_ref), (low_in, low_ref),
        (high_in, high_ref), (r3p_in, r3p_ref), (z3p_in, z3p_ref), (r5p_in, r5p_ref),
        (left5_in, left5_ref), (right5_in, right5_ref), (low5_in, low5_ref),
        (high5_in, high5_ref), (g5_in, g5_ref), (z5_in, z5_ref),
    ]
    moves = [pltpu.make_async_copy(a, b, sem.at[m]) for m, (a, b) in enumerate(moves)]
    for move in moves:
        move.start()

    def take3():
        for move in moves[1:7]:
            move.wait()
        refs = (left_ref, right_ref, low_ref, high_ref)
        unpack(4, 3, 4, 16, 4, r3p_ref, *refs, (0, 0), fl, r3_ref, True)
        unpack(4, 2, 4, 16, 4, z3p_ref, *refs, (X3R, Y3R), fl, z3_ref, False)

    def take5():
        for move in moves[7:12]:
            move.wait()
        refs = (left5_ref, right5_ref, low5_ref, high5_ref)
        unpack(6, 1, 2, 8, 2, r5p_ref, *refs, (0, 0), fl, r5_ref, True)
        moves[13].wait()

    m = interpolation(2, 4)
    moves[0].wait()

    def prolong1(a, carry):
        corner = [[[win_ref[a + i, pl.ds(j, 16), :]] for j in range(2)] for i in range(2)]
        along = [cs_apply(m, [corner[0][j][0], corner[1][j][0]]) for j in range(2)]
        for i in range(4):
            line = cs_apply(m, [along[0][i], along[1][i]])
            for j in range(4):
                v = cs_fold(m, [line[j]])
                for k in range(2):
                    g = ld(g3_ref, gslot(4, a, i, j, k), 16)
                    st(v3_ref, a * c3 + ix(4, i, j, k), 16, jnp.where(g > 0.0, v[k], 0.0))
        return carry

    lax.fori_loop(0, 12, prolong1, 0)

    def finish3(a, i, j, k, x):
        s = a * c3 + ix(4, i, j, k)
        st(z3_ref, s, 16, ld(z3_ref, s, 16) + x)

    up_smooth(4, 12, 16, v3_ref, r3_ref, g3_ref, u3_ref, t3_ref, a3_ref, take3, finish3)

    m5 = interpolation(4, 6)
    moves[12].wait()

    def prolong3(a, carry):
        for j in range(4):
            for k in range(2):
                src = []
                for i in range(4):
                    v = ld(z3_ref, (a + 2) * c3 + ix(4, i, j, k), 16)
                    src.append(v[2:10])
                line = cs_apply(m5, src)
                for i in range(6):
                    st(w1_ref, (i * 4 + j) * 2 + k, 8, line[i])
        for i in range(6):
            cols = []
            for k in range(2):
                cols.append(cs_apply(m5, [ld(w1_ref, (i * 4 + j) * 2 + k, 8) for j in range(4)]))
            for j in range(6):
                v = cs_fold(m5, [cols[k][j] for k in range(2)])
                for k in range(3):
                    g = ld(g5_ref, gslot(6, a, i, j, k), 8)
                    st(v5_ref, a * c5 + ix(6, i, j, k), 8, jnp.where(g > 0.0, v[k], 0.0))
        return carry

    lax.fori_loop(0, 8, prolong3, 0)

    def finish5(a, i, j, k, x):
        s = ix(6, i, j, k)
        v = ld(z5_ref, (a - 2) * c5 + s, 8) + x
        start = ((a - 2) * 6 + i) * 24 + j
        y_ref[pl.ds(576 * k + start, 4, stride=6), :] = v[2:6]

    up_smooth(6, 8, 8, v5_ref, r5_ref, g5_ref, u5_ref, t5_ref, a5_ref, take5, finish5)
    y = jnp.concatenate([y_ref[pl.ds(576 * k, 576), :] for k in range(3)], axis=1)
    out_ref[...] = exact_dot(y, perm_ref[...])


def class_maps(heights, gx, gy, ring, rows, r0):
    na, nb = heights.shape
    w = 4 + 2 * ring + 2
    pad = ((ring + 1, ring + 1), (ring + 1, ring + 1))
    start = (4 * gx, 4 * gy)
    h = lax.dynamic_slice(jnp.pad(heights, pad), start, (w, w))
    e = lax.dynamic_slice(jnp.pad(jnp.ones((na, nb), F32), pad), start, (w, w))
    ax = jnp.arange(w) + 4 * gx - ring - 1
    ay = jnp.arange(w) + 4 * gy - ring - 1
    fx = ((ax >= 0) & (ax < na)).astype(F32)
    fy = ((ay >= 0) & (ay < nb)).astype(F32)
    hx = jnp.stack([jnp.maximum(h[:-2], h[1:-1]), h[1:-1], jnp.maximum(h[1:-1], h[2:])], 1)
    hxy = jnp.stack(
        [
            jnp.maximum(hx[:, :, :-2], hx[:, :, 1:-1]),
            hx[:, :, 1:-1],
            jnp.maximum(hx[:, :, 1:-1], hx[:, :, 2:]),
        ],
        2,
    )
    own = e[1:-1, 1:-1][:, None, None, :]
    hxy = jnp.where(own > 0.0, hxy, 1000)

    def inv(f):
        return jnp.stack([1.0 / (1.0 + f[:-2]), jnp.ones_like(f[1:-1]), 1.0 / (1.0 + f[2:])], 1)

    exy = inv(fx)[:, :, None, None] * inv(fy).T[None, None, :, :]
    extra = rows - (w - 2)
    hxy = jnp.pad(hxy, ((0, 0), (0, 0), (0, 0), (0, extra)), constant_values=1000)
    exy = jnp.pad(exy, ((0, 0), (0, 0), (0, 0), (0, extra)))
    lane = jnp.arange(128)
    c = lane & 63
    bound = jnp.stack([jnp.where(lane < 64, c - 1, c), c])
    zfac = jnp.stack([jnp.where(lane == 127, 1.0, 0.5), jnp.ones(128)]).astype(F32)
    g = jnp.where(
        bound[None, None, None, :, None, :] >= hxy[:, :, :, None, :, None],
        exy[:, :, :, None, :, None] * zfac[None, None, None, :, None, :],
        0.0,
    )
    return g.reshape(-1, 128)


def coarse_weight(heights):
    na, nb = heights.shape
    h = jnp.pad(heights, 1)
    hn = jnp.maximum(h[:-1], h[1:])
    hn = jnp.maximum(hn[:, :-1], hn[:, 1:])
    half = na // 2
    hn = jnp.stack([hn[: half + 1], hn[half:][::-1]], 2)
    hn = jnp.pad(hn, ((0, 0), (0, 72 - nb - 1), (0, 0)), constant_values=1000)
    hn = jnp.repeat(hn, 64, axis=2)
    la = jnp.arange(half + 1)
    b = jnp.arange(72)
    kk = jnp.arange(128) & 63
    ex = jnp.where(la == 0, 1.0, 2.0)[:, None, None]
    ey = jnp.where((b == 0) | (b == nb), 1.0, 2.0)[None, :, None]
    ez = jnp.where(kk == 63, 1.0, 2.0)[None, None, :]
    return jnp.where(kk[None, None, :] >= hn, 0.5 * ex * ey * ez, 0.0).astype(F32)


def perm_in():
    m = np.zeros((384, 384), np.float32)
    for z in range(384):
        c, k = divmod(z, 6)
        m[z, k * 128 + c if k < 3 else (5 - k) * 128 + 64 + c] = 1.0
    return m


def perm_coarse():
    m = np.zeros((128, 128), np.float32)
    for c in range(64):
        m[c, 2 * c] = 1.0
        m[64 + c, 2 * c + 1] = 1.0
    return m


def call(kernel, outs, ins, scratch, out_specs=None):
    return pl.pallas_call(
        kernel,
        out_shape=[jax.ShapeDtypeStruct(s, F32) for s in outs],
        in_specs=ins,
        out_specs=out_specs or [VMEM] * len(outs),
        scratch_shapes=[pltpu.VMEM(s, F32) if isinstance(s, tuple) else s for s in scratch],
        compiler_params=pltpu.CompilerParams(vmem_limit_bytes=56 * 1024 * 1024),
    )


def both_ways(axis, to_low, to_high):
    n = lax.axis_size(axis)
    from_low = lax.ppermute(to_high, axis, [(i, (i + 1) % n) for i in range(n)])
    from_high = lax.ppermute(to_low, axis, [(i, (i - 1) % n) for i in range(n)])
    return from_low, from_high


def per_device(source, heights):
    gx, gy = lax.axis_index("gx"), lax.axis_index("gy")
    nx, ny = lax.axis_size("gx"), lax.axis_size("gy")
    ids = jnp.stack([gx, gy, nx, ny]).astype(jnp.int32)
    g5 = class_maps(heights, gx, gy, 2, 8, 2)
    g3d = class_maps(heights, gx, gy, 2, 8, 2)
    pin = jnp.asarray(perm_in(), jnp.bfloat16)
    pout = jnp.asarray(perm_in().T, jnp.bfloat16)
    pc = jnp.asarray(perm_coarse(), jnp.bfloat16)

    def f(n, a):
        return (a * per(n) * 8, 128)

    s5, b5p, ml, mr, lo, hi = call(
        layout_kernel,
        [f(6, 4), f(6, 4), (432, 128), (432, 128), (432, 128), (432, 128)],
        [VMEM] * 2,
        [(1872, 128), f(6, 6)],
    )(source.reshape(576, 384), pin)
    left, right = both_ways("gx", ml, mr)
    left, later = lax.optimization_barrier((left, heights))
    g3 = class_maps(later, gx, gy, 4, 16, 4)
    cw = coarse_weight(later)
    dn, up = call(
        functools.partial(y_lines_kernel, 6), [(648, 128)] * 2, [SMEM] + [VMEM] * 4, []
    )(ids, lo, hi, left, right)
    low, high = both_ways("gy", dn, up)
    low, g3, cw = lax.optimization_barrier((low, g3, cw))
    z5, r5p, m5l, m5r, lo5, hi5, s3, b3p, ml, mr, lo, hi = call(
        fine_down_kernel,
        [f(6, 4), f(6, 4)] + [(432, 128)] * 4 + [f(4, 4), f(4, 4)] + [(128, 128)] * 4,
        [SMEM, ANY] + [VMEM] * 6,
        [f(6, 6), f(6, 6), f(6, 6), f(6, 1), f(6, 1), f(6, 1), f(4, 6), f(6, 4), f(6, 4)]
        + [pltpu.SemaphoreType.DMA((2,))],
        [ANY] + [VMEM] * 11,
    )(ids, s5, b5p, left, right, low, high, g5)
    left, right = both_ways("gx", ml, mr)
    left5, right5 = both_ways("gx", m5l, m5r)
    dn, up = call(
        functools.partial(y_lines_kernel, 4), [(192, 128)] * 2, [SMEM] + [VMEM] * 4, []
    )(ids, lo, hi, left, right)
    low, high = both_ways("gy", dn, up)
    left5, dn = lax.optimization_barrier((left5, dn))
    dn5, up5 = call(
        functools.partial(y_lines_kernel, 6), [(648, 128)] * 2, [SMEM] + [VMEM] * 4, []
    )(ids, lo5, hi5, left5, right5)
    low, dn5, up5 = lax.optimization_barrier((low, dn5, up5))
    low5, high5 = both_ways("gy", dn5, up5)
    xr, yr = X3R + X3Z, Y3R + Y3Z
    z3, r3p, block, ml, mr = call(
        middle_down_kernel,
        [f(4, 4), f(4, 4), (nx * ny * 8, 128), (xr, 128), (xr, 128)],
        [SMEM] + [VMEM] * 7,
        [f(4, 6), f(4, 6), f(4, 6), f(4, 1), f(4, 1), f(4, 1), (64, 128)],
    )(ids, s3, b3p, left, right, low, high, g3d)
    every = block.reshape(nx * ny // 2, 16, 128)
    groups = [[(2 * x + c) * ny + y for x in range(nx // 2) for y in range(ny)] for c in range(2)]
    same = lax.all_to_all(every, ("gx", "gy"), 0, 0, axis_index_groups=groups)
    same = same.reshape(nx * ny * 8, 128)
    other = lax.ppermute(same, "gx", [(i, i ^ 1) for i in range(nx)])
    left, right = both_ways("gx", ml, mr)
    left, low5, high5 = lax.optimization_barrier((left, low5, high5))
    dn, up = call(up_lines_kernel, [(yr, 128)] * 2, [SMEM] + [VMEM] * 4, [])(
        ids, r3p, z3, left, right
    )
    low, high = both_ways("gy", dn, up)
    win, coarse = call(
        coarse_kernel,
        [(13, 24, 128), (64, 128)],
        [SMEM] + [VMEM] * 4,
        [(17, 88, 128)] * 4 + [(64, 128)],
    )(ids, same, other, cw, pc)

    def f16(a):
        return (a * per(4) * 16, 128)

    (out,) = call(
        up_kernel,
        [(576, 384)],
        [SMEM, VMEM] + [ANY] * 14 + [VMEM],
        [f(6, 4), f(6, 4), f(4, 4), f(4, 4), (xr, 128), (xr, 128), (yr, 128), (yr, 128)]
        + [(432, 128), (432, 128), (648, 128), (648, 128)]
        + [(8 * 18 * 8, 128), (12 * 18 * 16, 128), pltpu.SemaphoreType.DMA((14,)), f16(12), f16(12), f16(12), f16(12), f16(12), f16(1)]
        + [f(6, 8), f(6, 8), f(6, 8), f(6, 8), f(6, 1), f(6, 1), f(6, 1), (1728, 128)],
    )(
        ids, win, r5p, z5, r3p, z3, left, right, low, high, left5, right5, low5, high5, g5, g3, pout
    )
    return out.reshape(24, 24, 384), coarse.reshape(8, 8, 128)


def solution(mesh):
    spec = P("gx", "gy", None)
    return jax.shard_map(
        per_device, mesh=mesh, in_specs=(spec, P()), out_specs=(spec, spec), check_vma=False
    )
```
